32 devices in a mesh: ctx: 16 (over z, x, core), fsdp: 2 (over y).
Axes of the slice: x: 2, y: 2, z: 4, core: 2. Of those that a mesh axis runs over, the one named last changes fastest.
Arguments:
- inputs: bfloat16 [4, 1024, 1024], P('fsdp', 'ctx'), may hold values from -6 to 6
- gain_attn: bfloat16 [1024], P(('ctx', 'fsdp')), may hold values from 0.25 to 1.75
- gain_mlp: bfloat16 [1024], P(('ctx', 'fsdp')), may hold values from 0.25 to 1.75
- w_qkv: bfloat16 [1024, 3072], P(('ctx', 'fsdp')), may hold values from -0.1875 to 0.1875
- w_attn_out: bfloat16 [1024, 1024], P(('ctx', 'fsdp')), may hold values from -3.5 to 3.5
- w_in: bfloat16 [1024, 5248], P(('ctx', 'fsdp')), may hold values from -0.1875 to 0.1875
- w_out: bfloat16 [2624, 1024], P(None, ('ctx', 'fsdp')), may hold values from -0.125 to 0.125
- cotangent: bfloat16 [4, 1024, 1024], P('fsdp', 'ctx'), may hold values from -6 to 6
Outputs:
- output: bfloat16 [4, 1024, 1024], P('fsdp', 'ctx')
- input_grad: float32 [4, 1024, 1024], P('fsdp', 'ctx')
- grad_gain_attn: float32 [1024], P(('ctx', 'fsdp'))
- grad_gain_mlp: float32 [1024], P(('ctx', 'fsdp'))
- grad_qkv: float32 [1024, 3072], P(('ctx', 'fsdp'))
- grad_attn_out: float32 [1024, 1024], P(('ctx', 'fsdp'))
- grad_in: float32 [1024, 5248], P(('ctx', 'fsdp'))
- grad_out: float32 [2624, 1024], P(None, ('ctx', 'fsdp'))
The draws below stay inside these ranges and needn't reach their ends.
All inputs are finite; a program needn't handle non-finite values.
Results may differ from the reference program's by a relative error of at most 0.035.
Values may be sent and summed in bfloat16 or wider, within the bound.
No kernel may reach another device: no remote copies, remote signals or barrier semaphores. Data moves between devices by JAX's collectives and lax.ppermute only.
A program may use at most 320 MiB of HBM per device.

```python
import math
import jax
import jax.numpy as jnp
from jax import lax

D = 1024
HEADS = 16
HEAD_DIM = 64
FF = 2624
LENGTH = 1024
SEQS = 4


def spiked(array, stream_key, source, target, blocks, factor):
    def block_of(axis_at):
        return (jnp.arange(array.shape[axis_at]) // (array.shape[axis_at] // blocks)).reshape((-1,) + (1,) * (array.ndim - 1 - axis_at))

    near = jax.random.permutation(stream_key, blocks)[block_of(target)]
    other_side = (block_of(target) + blocks // 2) % blocks
    return jnp.where((block_of(source) == near) | (block_of(source) == other_side), factor * array, array)


def levels(stream_key, extent, pieces, smallest, largest):
    loudness, own = 1.0, jax.random.fold_in(stream_key, 6)
    for position, blocks in pieces:
        steps = jnp.exp(jax.random.uniform(jax.random.fold_in(own, position), (blocks,), jnp.float32, smallest / len(pieces), largest / len(pieces)))
        loudness = loudness * jnp.repeat(steps, extent[position] // blocks).reshape([-1 if axis == position else 1 for axis in range(len(extent))])
    return loudness


def bell_draw(key, shape, scale, most, split=(), kind=jnp.bfloat16):
    values = jax.random.normal(key, shape, jnp.float32) * scale
    if len(split) > 0:
        values = levels(key, shape, split, -0.22, 0.18) * values
    return jnp.clip(values, min=-most, max=most).astype(kind)


def gaussian_with(stream_key, shape, scale, bound, shards, heavy, kind=jnp.bfloat16):
    values = scale * jax.random.normal(stream_key, shape, jnp.float32)
    if shards:
        values = values * levels(stream_key, shape, shards, -0.22, 0.18)
    return jnp.clip(spiked(values, jax.random.fold_in(stream_key, 3), *heavy), -bound, bound).astype(kind)


def setup_inputs(seed: int = 0) -> dict:
    streams_of = jax.random.split(jax.random.key(seed), 9)
    return {
        "inputs": bell_draw(streams_of[0], (SEQS, LENGTH, D), 1.0, 6.0, ((0, 2), (1, 16))),
        "gain_attn": jnp.clip(1.0 + 0.15 * jax.random.normal(streams_of[1], (D,), jnp.float32), 0.25, 1.75).astype(jnp.bfloat16),
        "gain_mlp": jnp.clip(1.0 + 0.15 * jax.random.normal(streams_of[2], (D,), jnp.float32), 0.25, 1.75).astype(jnp.bfloat16),
        "w_qkv": bell_draw(streams_of[3], (D, 3 * D), D ** -0.5, 0.1875, ((0, 32),)),
        "w_attn_out": bell_draw(streams_of[4], (D, D), (max(1, 3 * D // LENGTH)) ** -0.5, 3.5, ((0, 32),)),
        "w_in": bell_draw(streams_of[5], (D, 2 * FF), D ** -0.5, 0.1875, ((0, 32),)),
        "w_out": bell_draw(streams_of[6], (FF, D), FF ** -0.5, 0.125, ((1, 32),)),
        "cotangent": gaussian_with(streams_of[7], (SEQS, LENGTH, D), 1.0, 6.0, ((0, 2), (1, 16)), (1, 2, 16, 2.0)),
    }


norm_eps = 1e-05
rope_base = 160000.0
query_block = 512

@jax.custom_vjp
def low(v):
    return lax.optimization_barrier(v.astype(jnp.bfloat16)).astype(jnp.float32)

@jax.custom_vjp
def low_back(v):
    return v

def low_keep(v):
    return (low(v), None)

def low_pass(kept, grad):
    return (grad,)

def back_keep(v):
    return (v, None)

def back_low(kept, grad):
    return (low(grad),)
low.defvjp(low_keep, low_pass)
low_back.defvjp(back_keep, back_low)

def product(left_side, right_side):
    return jnp.dot(left_side, right_side, precision=lax.Precision.HIGHEST)

def layer_norm(values, gain):
    centre = values - lax.optimization_barrier(jnp.mean(values, axis=-1, keepdims=True))
    spread = lax.optimization_barrier(jnp.mean(centre * centre, axis=-1, keepdims=True))
    return centre * lax.rsqrt(spread + norm_eps) * gain

def rotary(heads_in):
    halfway = HEAD_DIM // 2
    places = jnp.arange(LENGTH, dtype=jnp.int32).astype(jnp.float32)
    inverse = rope_base ** (-2.0 * jnp.arange(halfway, dtype=jnp.int32).astype(jnp.float32) / HEAD_DIM)
    angles = places[:, None] * inverse[None, :]
    cosine = jnp.cos(angles)[:, None, :]
    sine_table = jnp.sin(angles)[:, None, :]
    first_half = heads_in[..., :halfway]
    second_half = heads_in[..., halfway:]
    return jnp.concatenate([first_half * cosine - second_half * sine_table, second_half * cosine + first_half * sine_table], axis=-1)

def attend_rows(query_rows, key_heads, value_heads):
    scores = jnp.einsum('qhd,khd->qhk', query_rows, key_heads, precision=lax.Precision.HIGHEST) * HEAD_DIM ** (-0.5)
    scores = low_back(scores)
    shifted = scores - lax.optimization_barrier(jnp.max(scores, axis=-1, keepdims=True))
    weights = jnp.exp(shifted)
    probability = weights / lax.optimization_barrier(jnp.sum(weights, axis=-1, keepdims=True))
    return jnp.einsum('qhk,khd->qhd', low(probability), value_heads, precision=lax.Precision.HIGHEST)

def attend_sequence(triple):
    query_heads, key_heads, value_heads = triple
    row_count = math.gcd(LENGTH, query_block)
    grouped = query_heads.reshape(LENGTH // row_count, row_count, HEADS, HEAD_DIM)
    blockwise = jax.checkpoint(lambda member: attend_rows(member, key_heads, value_heads))
    return lax.map(blockwise, grouped).reshape(LENGTH, HEADS, HEAD_DIM)

def forward(tokens_in, gain_attn, gain_mlp, w_qkv, w_attn_out, w_in, w_out):
    normed_one = low(layer_norm(tokens_in, gain_attn))
    projected = low_back(product(normed_one, w_qkv))
    split_shape = (SEQS, LENGTH, HEADS, HEAD_DIM)
    query_heads = low(rotary(projected[..., :D].reshape(split_shape)))
    key_heads = low(rotary(projected[..., D:2 * D].reshape(split_shape)))
    value_heads = low(projected[..., 2 * D:].reshape(split_shape))
    attention = lax.map(attend_sequence, (query_heads, key_heads, value_heads))
    attended = low(low_back(attention.reshape(SEQS, LENGTH, D)))
    middle = tokens_in + low_back(product(attended, w_attn_out))
    normed_two = low(layer_norm(middle, gain_mlp))
    gate_up = low_back(product(normed_two, w_in))
    hidden = low(jax.nn.gelu(gate_up[..., :FF], approximate=False) * gate_up[..., FF:])
    return middle + low_back(product(hidden, w_out))

def reference(inputs, gain_attn, gain_mlp, w_qkv, w_attn_out, w_in, w_out, cotangent):
    arrays = [member.astype(jnp.float32) for member in (inputs, gain_attn, gain_mlp, w_qkv, w_attn_out, w_in, w_out)]
    result, pullback = jax.vjp(forward, *arrays)
    gradients = pullback(cotangent.astype(jnp.float32))
    return (result.astype(jnp.bfloat16), gradients[0], gradients[1], gradients[2], gradients[3], gradients[4], gradients[5], gradients[6])
```

```python
import functools
import math

import jax
import jax.numpy as jnp
from jax import lax
from jax.experimental import pallas as pl
from jax.experimental.pallas import tpu as pltpu
from jax.sharding import Mesh
from jax.sharding import PartitionSpec as P

HEADS = 16
norm_eps = 1e-05
rope_base = 160000.0
f32 = jnp.float32
bf16 = jnp.bfloat16
LANES = 128
MIB = 1024 * 1024


def partner(array, axis, step=1):
    size = lax.axis_size(axis)
    return lax.ppermute(array, axis, [(i, i ^ step) for i in range(size)])


def opposite(array):
    return lax.ppermute(array, ("x", "y"), [(i, 3 - i) for i in range(4)])


def paired(own, other, place, axis):
    first = jnp.where(place == 0, own, other)
    second = jnp.where(place == 0, other, own)
    return jnp.stack([first, second], axis=axis)


def core_swap(array):
    place = lax.axis_index("c")
    kept = lax.dynamic_index_in_dim(array, place, 0, False)
    sent = lax.dynamic_index_in_dim(array, 1 - place, 0, False)
    return paired(kept, partner(sent, "c"), place, 0)


def gather_chips(block):
    zi, xi = lax.axis_index("z"), lax.axis_index("x")
    pieces = [block] + [partner(block, "z", j) for j in range(1, 4)]
    whole = jnp.zeros((4, 2) + block.shape, block.dtype)
    rest = (0,) * block.ndim
    for j, piece in enumerate(pieces):
        across = partner(piece, "x")
        whole = lax.dynamic_update_slice(whole, piece[None, None], (zi ^ j, xi) + rest)
        whole = lax.dynamic_update_slice(whole, across[None, None], (zi ^ j, 1 - xi) + rest)
    return whole


def scatter_chips(terms):
    zi, xi = lax.axis_index("z"), lax.axis_index("x")

    def block(j, other):
        at = (zi ^ j, xi ^ other) + (0,) * (terms.ndim - 2)
        return lax.dynamic_slice(terms, at, (1, 1) + terms.shape[2:])[0, 0]

    total = None
    for j in (2, 3, 1, 0):
        part = block(j, 0).astype(f32) + partner(block(j, 1), "x").astype(f32)
        if j:
            part = partner(part.astype(terms.dtype), "z", j).astype(f32)
        total = part if total is None else total + part
    return total


def gather_plane(block):
    over_x = partner(block, "x")
    over_y = partner(block, "y")
    over_both = partner(over_y, "x")
    here = jnp.stack([block, over_x, over_y, over_both])
    return jnp.stack([here, partner(here, "c")])


def scatter_plane(terms):
    chip = (terms[0].astype(f32) + partner(terms[1], "c").astype(f32)).astype(terms.dtype)
    over_x = partner(chip[1], "x")
    over_y = partner(chip[2], "y")
    over_both = opposite(chip[3])
    return (
        chip[0].astype(f32)
        + over_x.astype(f32)
        + over_y.astype(f32)
        + over_both.astype(f32)
    )


def nt(left, right):
    return lax.dot_general(left, right, (((1,), (1,)), ((), ())), preferred_element_type=f32)


def tn(left, right):
    return lax.dot_general(left, right, (((0,), (0,)), ((), ())), preferred_element_type=f32)


def nn(left, right):
    return lax.dot_general(left, right, (((1,), (0,)), ((), ())), preferred_element_type=f32)


def halves_swapped(values, half):
    lane = lax.broadcasted_iota(jnp.int32, values.shape, 1)
    up = pltpu.roll(values, half, 1)
    down = pltpu.roll(values, values.shape[1] - half, 1)
    return jnp.where(lane % (2 * half) < half, down, up)


def project_kernel(half, tokens_ref, weight_ref, cos_ref, sin_ref, q_ref, k_ref, v_ref):
    width = q_ref.shape[1]
    made = nn(tokens_ref[...], weight_ref[...])
    cosine, sine = cos_ref[...], sin_ref[...]
    for place, ref in ((0, q_ref), (1, k_ref)):
        part = made[:, place * width : (place + 1) * width]
        ref[...] = (part * cosine + halves_swapped(part, half) * sine).astype(bf16)
    v_ref[...] = made[:, 2 * width :].astype(bf16)


def project(tokens, weight, cosine, sine, half):
    rows, depth = tokens.shape
    width = weight.shape[1] // 3
    step = math.gcd(rows, 256)
    by_row = lambda w: pl.BlockSpec((step, w), lambda i: (i, 0))
    return pl.pallas_call(
        functools.partial(project_kernel, half),
        grid=(rows // step,),
        in_specs=[
            by_row(depth),
            pl.BlockSpec((depth, 3 * width), lambda i: (0, 0)),
            by_row(width),
            by_row(width),
        ],
        out_specs=[by_row(width)] * 3,
        out_shape=[jax.ShapeDtypeStruct((rows, width), bf16)] * 3,
        compiler_params=pltpu.CompilerParams(vmem_limit_bytes=24 * MIB),
        name="project",
    )(tokens, weight, cosine, sine)


def of_head(values, head, size):
    lane = lax.broadcasted_iota(jnp.int32, values.shape, 1)
    return jnp.where(lane // size == head, values, jnp.zeros_like(values))


def attend_kernel(size, scale, q_ref, k_ref, v_ref, o_ref, log_ref):
    keys, values, queries = k_ref[...], v_ref[...], q_ref[...]
    outs = []
    for head in range(q_ref.shape[1] // size):
        scores = nt(keys, of_head(queries, head, size))
        top = jnp.max(scores, axis=0, keepdims=True)
        weights = jnp.exp2((scores - top) * scale)
        total = jnp.sum(weights, axis=0, keepdims=True)
        probs = (weights * (1.0 / total)).astype(bf16)
        outs.append(tn(values, probs)[head * size : (head + 1) * size])
        log_ref[head : head + 1, :] = top * scale + jnp.log2(total)
    o_ref[...] = jnp.transpose(jnp.concatenate(outs, axis=0)).astype(bf16)


def attend(queries, keys, values, size):
    rows, width = queries.shape
    count = keys.shape[0]
    step = math.gcd(rows, 256 if count <= 2048 else 128)
    scale = math.log2(math.e) / math.sqrt(size)
    by_row = pl.BlockSpec((step, width), lambda i: (i, 0))
    whole = pl.BlockSpec((count, width), lambda i: (0, 0))
    return pl.pallas_call(
        functools.partial(attend_kernel, size, scale),
        grid=(rows // step,),
        in_specs=[by_row, whole, whole],
        out_specs=[by_row, pl.BlockSpec((8, step), lambda i: (0, i))],
        out_shape=[
            jax.ShapeDtypeStruct((rows, width), bf16),
            jax.ShapeDtypeStruct((8, rows), f32),
        ],
        compiler_params=pltpu.CompilerParams(vmem_limit_bytes=40 * MIB),
        name="attend",
    )(queries, keys, values)


def attend_back_kernel(
    size, scale, q_ref, k_ref, v_ref, grad_ref, log_ref, dq_ref, dk_ref, dv_ref
):
    @pl.when(pl.program_id(0) == 0)
    def _():
        dk_ref[...] = jnp.zeros_like(dk_ref)
        dv_ref[...] = jnp.zeros_like(dv_ref)

    keys, values, queries, grads = k_ref[...], v_ref[...], q_ref[...], grad_ref[...]
    exponent = scale * math.log2(math.e)
    outs = []
    for head in range(q_ref.shape[1] // size):
        query, grad = of_head(queries, head, size), of_head(grads, head, size)
        probs = jnp.exp2(nt(keys, query) * exponent - log_ref[head : head + 1, :])
        grad_probs = nt(values, grad)
        delta = jnp.sum(probs * grad_probs, axis=0, keepdims=True)
        grad_scores = (probs * (grad_probs - delta)).astype(bf16)
        outs.append(tn(keys, grad_scores)[head * size : (head + 1) * size])
        dk_ref[...] += nn(grad_scores, query) * scale
        dv_ref[...] += nn(probs.astype(bf16), grad)
    dq_ref[...] = jnp.transpose(jnp.concatenate(outs, axis=0)) * scale


def attend_back(queries, keys, values, grads, logs, size):
    rows, width = queries.shape
    count = keys.shape[0]
    step = math.gcd(rows, 256 if count <= 2048 else 128)
    by_row = pl.BlockSpec((step, width), lambda i: (i, 0))
    whole = pl.BlockSpec((count, width), lambda i: (0, 0))
    return pl.pallas_call(
        functools.partial(attend_back_kernel, size, 1.0 / math.sqrt(size)),
        grid=(rows // step,),
        in_specs=[by_row, whole, whole, by_row, pl.BlockSpec((8, step), lambda i: (0, i))],
        out_specs=[by_row, whole, whole],
        out_shape=[
            jax.ShapeDtypeStruct((rows, width), f32),
            jax.ShapeDtypeStruct((count, width), f32),
            jax.ShapeDtypeStruct((count, width), f32),
        ],
        compiler_params=pltpu.CompilerParams(vmem_limit_bytes=52 * MIB),
        name="attend_back",
    )(queries, keys, values, grads, logs)


def turn_back_kernel(half, dq_ref, dk_ref, dv_ref, cos_ref, sin_ref, out_ref):
    width = dq_ref.shape[1]
    cosine, sine = cos_ref[...], sin_ref[...]
    for place, ref in ((0, dq_ref), (1, dk_ref)):
        part = ref[...]
        turned = part * cosine - halves_swapped(part, half) * sine
        out_ref[:, place * width : (place + 1) * width] = turned.astype(bf16)
    out_ref[:, 2 * width :] = dv_ref[...].astype(bf16)


def turn_back(dq, dk, dv, cosine, sine, half):
    rows, width = dq.shape
    return pl.pallas_call(
        functools.partial(turn_back_kernel, half),
        out_shape=jax.ShapeDtypeStruct((rows, 3 * width), bf16),
        compiler_params=pltpu.CompilerParams(vmem_limit_bytes=24 * MIB),
        name="turn_back",
    )(dq, dk, dv, cosine, sine)


def normalize(values):
    centre = values - jnp.mean(values, axis=-1, keepdims=True)
    inverse = lax.rsqrt(jnp.mean(centre * centre, axis=-1, keepdims=True) + norm_eps)
    return centre * inverse, inverse


def normalize_back(scaled, normed, inverse):
    inner = jnp.mean(scaled * normed, axis=-1, keepdims=True)
    return inverse * (scaled - jnp.mean(scaled, axis=-1, keepdims=True) - normed * inner)


def columns_by(array, pieces, piece):
    rows, count = array.shape
    padded = jnp.pad(array, ((0, 0), (0, pieces * piece - count)))
    return jnp.swapaxes(padded.reshape(rows, pieces, piece), 0, 1)


def columns_back(array, count):
    pieces, rows, piece = array.shape
    return jnp.swapaxes(array, 0, 1).reshape(rows, pieces * piece)[:, :count]


def body(inputs, gain_attn, gain_mlp, w_qkv, w_attn_out, w_in, w_out, cotangent):
    pairs, planes = 8, 8
    rings = lax.axis_size("r")
    ci, yi, ri = (lax.axis_index(name) for name in "cyr")
    seqs, half_block, width = inputs.shape
    owned = w_qkv.shape[0]
    size = width // HEADS
    half = size // 2
    wide = width // pairs
    block = seqs * half_block
    span = pairs * block
    ff = w_out.shape[0]
    piece = -(-ff // (planes * LANES)) * LANES

    gain_one = gain_attn.astype(f32)[:, None]
    gain_two = gain_mlp.astype(f32)[:, None]

    tokens = core_swap(inputs).reshape(block, width).astype(f32)
    cotangent_here = core_swap(cotangent).reshape(block, width)
    normed_one, inverse_one = normalize(tokens)
    all_one = gather_chips(normed_one.astype(bf16)).reshape(span, width)

    scaled_qkv = (w_qkv.astype(f32) * gain_one).astype(bf16)
    part = scaled_qkv.reshape(owned, 3, pairs, wide).transpose(2, 0, 1, 3)
    part = part.reshape(pairs, owned, 3 * wide)
    part = lax.all_to_all(part, ("z", "x"), 0, 0, tiled=True)
    part = paired(part, partner(part, "c"), ci, 1)
    part = paired(part, partner(part, "y"), yi, 2)
    pair_qkv = lax.all_gather(part, "r", axis=0) if rings > 1 else part
    pair_qkv = pair_qkv.reshape(width, 3 * wide)

    full_attn = lax.all_gather(w_attn_out, ("r", "z", "x", "c", "y"), axis=0, tiled=True)

    scaled_in = (w_in.astype(f32) * gain_two).astype(bf16)
    turned_out = jnp.transpose(w_out)
    packed = jnp.concatenate(
        [
            columns_by(scaled_in[:, :ff], planes, piece),
            columns_by(scaled_in[:, ff:], planes, piece),
            columns_by(turned_out, planes, piece),
        ],
        axis=2,
    )
    packed = lax.all_to_all(packed, ("x", "c", "y"), 0, 0, tiled=True)
    packed = packed.reshape(planes * owned, 3 * piece)
    packed = lax.all_gather(packed, ("r", "z"), axis=0, tiled=True)
    part_in, part_out = packed[:, : 2 * piece], packed[:, 2 * piece :]

    all_cotangent = gather_plane(cotangent_here).reshape(planes * block, width)

    places = (ri * span + jnp.arange(span, dtype=jnp.int32)).astype(f32)
    frequency = rope_base ** (-2.0 * jnp.arange(half, dtype=jnp.int32).astype(f32) / size)
    angles = places[:, None] * frequency[None, :]
    cosine = jnp.tile(jnp.cos(angles), (1, wide // half))
    sine = jnp.sin(angles)
    sine = jnp.tile(jnp.concatenate([-sine, sine], axis=1), (1, wide // size))
    queries, keys, values = project(all_one, pair_qkv, cosine, sine, half)
    if rings > 1:
        keys = lax.all_gather(keys, "r", axis=0, tiled=True)
        values = lax.all_gather(values, "r", axis=0, tiled=True)
    heads_out, logs = attend(queries, keys, values, size)
    arrived = lax.all_to_all(heads_out.reshape(pairs, block, wide), ("z", "x"), 0, 0, tiled=True)
    attended = jnp.swapaxes(arrived, 0, 1).reshape(block, width)

    middle = tokens + nn(attended, full_attn)
    normed_two, inverse_two = normalize(middle)
    all_two = gather_plane(normed_two.astype(bf16)).reshape(planes * block, width)

    gate_up = nn(all_two, part_in)
    grad_hidden = nt(all_cotangent, part_out.T)
    gate, lift = gate_up[:, :piece], gate_up[:, piece:]
    cdf = 0.5 * (1.0 + lax.erf(gate * math.sqrt(0.5)))
    density = jnp.exp(-0.5 * gate * gate) * (1.0 / math.sqrt(2.0 * math.pi))
    activated = gate * cdf
    hidden = (activated * lift).astype(bf16)
    grad_gate_up = jnp.concatenate(
        [grad_hidden * lift * (cdf + gate * density), grad_hidden * activated], axis=1
    ).astype(bf16)
    plane_shape = (2, 4, block, width)
    grad_two = scatter_plane(nt(grad_gate_up, part_in).astype(bf16).reshape(plane_shape))
    result = scatter_plane(nt(hidden, part_out).astype(bf16).reshape(plane_shape))
    output = core_swap((middle + result).astype(bf16).reshape(seqs, half_block, width))

    grad_packed = jnp.concatenate([tn(all_two, grad_gate_up), tn(all_cotangent, hidden)], axis=1)
    grad_packed = lax.psum_scatter(
        grad_packed.astype(bf16), ("r", "z"), scatter_dimension=0, tiled=True
    )
    grad_packed = lax.all_to_all(
        grad_packed.reshape(planes, owned, 3 * piece), ("x", "c", "y"), 0, 0, tiled=True
    ).astype(f32)
    grad_in = jnp.concatenate(
        [
            columns_back(grad_packed[:, :, :piece], ff),
            columns_back(grad_packed[:, :, piece : 2 * piece], ff),
        ],
        axis=1,
    )
    grad_out = jnp.transpose(columns_back(grad_packed[:, :, 2 * piece :], ff))
    grad_gain_mlp = jnp.sum(grad_in * w_in.astype(f32), axis=1)
    grad_in = grad_in * gain_two

    grad_middle = cotangent_here.astype(f32) + normalize_back(grad_two, normed_two, inverse_two)
    grad_branch = grad_middle.astype(bf16)

    grad_attended = nt(grad_branch, full_attn).astype(bf16)
    leaving = jnp.swapaxes(grad_attended.reshape(block, pairs, wide), 0, 1)
    grad_heads = lax.all_to_all(leaving, ("z", "x"), 0, 0, tiled=True).reshape(span, wide)

    terms = tn(attended, grad_branch).astype(bf16)
    if rings > 1:
        terms = lax.psum_scatter(terms, "r", scatter_dimension=0, tiled=True)
    terms = terms.reshape(pairs, 2, 2, owned, width)
    grad_attn = sum_square(terms)
    grad_attn = scatter_chips(grad_attn.reshape(4, 2, owned, width))

    grad_q, grad_k, grad_v = attend_back(queries, keys, values, grad_heads, logs, size)
    if rings > 1:
        grad_k = lax.psum_scatter(grad_k, "r", scatter_dimension=0, tiled=True)
        grad_v = lax.psum_scatter(grad_v, "r", scatter_dimension=0, tiled=True)
    grad_projected = turn_back(grad_q, grad_k, grad_v, cosine, sine, half)

    grad_one = nt(grad_projected, pair_qkv).astype(bf16)
    grad_one = scatter_chips(grad_one.reshape(4, 2, block, width))
    input_grad = grad_middle + normalize_back(grad_one, normed_one, inverse_one)
    input_grad = core_swap(input_grad.reshape(seqs, half_block, width))

    terms = tn(all_one, grad_projected).astype(bf16)
    if rings > 1:
        terms = lax.psum_scatter(terms, "r", scatter_dimension=0, tiled=True)
    terms = sum_square(terms.reshape(pairs, 2, 2, owned, 3 * wide))
    terms = lax.all_to_all(terms, ("z", "x"), 0, 0, tiled=True).astype(f32)
    grad_qkv = terms.reshape(pairs, owned, 3, wide).transpose(1, 2, 0, 3).reshape(owned, 3 * width)
    grad_gain_attn = jnp.sum(grad_qkv * w_qkv.astype(f32), axis=1)
    grad_qkv = grad_qkv * gain_one
    return (
        output,
        input_grad,
        grad_gain_attn,
        grad_gain_mlp,
        grad_qkv,
        grad_attn,
        grad_in,
        grad_out,
    )


def sum_square(terms):
    ci, yi = lax.axis_index("c"), lax.axis_index("y")

    def member(array, place):
        return lax.dynamic_index_in_dim(array, place, 1, False)

    own = member(terms, ci).astype(f32)
    terms = (own + partner(member(terms, 1 - ci), "c").astype(f32)).astype(terms.dtype)
    own = member(terms, yi).astype(f32)
    return (own + partner(member(terms, 1 - yi), "y").astype(f32)).astype(terms.dtype)


def solution(mesh):
    ctx, fsdp = mesh.shape["ctx"], mesh.shape["fsdp"]
    grid = Mesh(mesh.devices.reshape(ctx // 16, 4, 2, 2, fsdp), ("r", "z", "x", "c", "y"))
    tokens = P("y", ("r", "z", "x", "c"), None)
    everyone = ("r", "z", "x", "c", "y")
    gain, rows, columns = P(everyone), P(everyone, None), P(None, everyone)
    return jax.shard_map(
        body,
        mesh=grid,
        in_specs=(tokens, gain, gain, rows, rows, rows, columns, tokens),
        out_specs=(tokens, tokens, gain, gain, rows, rows, rows, columns),
        check_vma=False,
    )
```

```python
import functools
import math

import jax
import jax.numpy as jnp
from jax import lax
from jax.experimental import pallas as pl
from jax.experimental.pallas import tpu as pltpu
from jax.sharding import Mesh
from jax.sharding import PartitionSpec as P

HEADS = 16
norm_eps = 1e-05
rope_base = 160000.0
f32 = jnp.float32
bf16 = jnp.bfloat16
LANES = 128
MIB = 1024 * 1024


def partner(array, axis):
    return lax.ppermute(array, axis, [(0, 1), (1, 0)])


def opposite(array, axes):
    return lax.ppermute(array, axes, [(i, 3 - i) for i in range(4)])


def after(array, *others):
    return lax.optimization_barrier((array, *others))[0]


def gather_chips(block):
    far = partner(block, "zh")
    near = partner(block, "zl")
    across = partner(block, "x")
    near_across = partner(near, "x")
    both = partner(far, "zl")
    far_across = partner(far, "x")
    both_across = partner(both, "x")
    return [block, across, near, near_across, far, far_across, both, both_across]


def add(*terms):
    total = terms[0].astype(f32)
    for term in terms[1:]:
        total = total + term.astype(f32)
    return total.astype(terms[0].dtype)


def scatter_chips(terms):
    across = {j: partner(terms[j ^ 1], "x") for j in (6, 4, 2, 0)}
    both = partner(add(terms[6], across[6]), "zl")
    near = partner(add(terms[2], across[2]), "zl")
    far = partner(add(terms[4], across[4], both), "zh")
    return terms[0], across[0], near, far


def gather_square(block):
    over_x = partner(block, "x")
    over_z = partner(block, "zl")
    over_both = opposite(block, ("zl", "x"))
    here = [block, over_x, over_z, over_both]
    return here + [partner(piece, "c") for piece in here]


def scatter_square(terms):
    there = [partner(piece, "c") for piece in terms[4:]]
    over_both = opposite(add(terms[3], there[3]), ("zl", "x"))
    over_x = partner(add(terms[1], there[1]), "x")
    over_z = partner(add(terms[2], there[2]), "zl")
    return terms[0], there[0], over_x, over_z, over_both


def call(kernel, name, outs, places, *arrays, scratch=(), mib=16):
    vmem = pl.BlockSpec(memory_space=pltpu.VMEM)
    return pl.pallas_call(
        kernel,
        in_specs=[pl.BlockSpec(memory_space=pltpu.SMEM)] + [vmem] * len(arrays),
        out_specs=[vmem] * len(outs),
        out_shape=[jax.ShapeDtypeStruct(shape, dtype) for shape, dtype in outs],
        scratch_shapes=list(scratch),
        compiler_params=pltpu.CompilerParams(vmem_limit_bytes=mib * MIB),
        name=name,
    )(places, *arrays)


CHIP, ZH, ZL, X, C, Y = range(6)


def nt(left, right):
    return lax.dot_general(left, right, (((1,), (1,)), ((), ())), preferred_element_type=f32)


def tn(left, right):
    return lax.dot_general(left, right, (((0,), (0,)), ((), ())), preferred_element_type=f32)


def nn(left, right):
    return lax.dot_general(left, right, (((1,), (0,)), ((), ())), preferred_element_type=f32)


def normalize(values):
    centre = values - jnp.mean(values, axis=-1, keepdims=True)
    inverse = lax.rsqrt(jnp.mean(centre * centre, axis=-1, keepdims=True) + norm_eps)
    return centre * inverse, inverse


def normalize_back(scaled, normed, inverse):
    inner = jnp.mean(scaled * normed, axis=-1, keepdims=True)
    return inverse * (scaled - jnp.mean(scaled, axis=-1, keepdims=True) - normed * inner)


def pick_kernel(places, own_ref, other_ref, block_ref):
    half = own_ref.shape[1]
    block_ref[:half, :] = own_ref[places[C]]
    block_ref[half:, :] = other_ref[places[C]]


def enter_kernel(places, own_ref, other_ref, block_ref, low_ref):
    pick_kernel(places, own_ref, other_ref, block_ref)
    low_ref[...] = normalize(block_ref[...].astype(f32))[0].astype(bf16)


def leave_kernel(places, own_ref, other_ref, out_ref):
    out_ref[places[C]] = own_ref[...]
    out_ref[1 - places[C]] = other_ref[...]


def assemble_kernel(lead, first, second, places, a_ref, b_ref, c_ref, d_ref, out_ref):
    chip = places[lead] if lead is not None else 0
    one, two = places[first], places[second]
    for i, row in enumerate(((a_ref, b_ref), (c_ref, d_ref))):
        for j, ref in enumerate(row):
            for at in range(ref.shape[0]):
                out_ref[chip ^ at, one ^ i, :, two ^ j] = ref[at]


def assemble(places, lead, first, second, pieces):
    extent = pieces[0].shape
    shape = (extent[0], 2, extent[1], 2) + extent[2:]
    if extent[2] % 16 == 0:
        kernel = functools.partial(assemble_kernel, lead, first, second)
        return call(kernel, "assemble", [(shape, bf16)], places, *pieces)[0]

    def ordered(own, other, place, axis):
        straight = jnp.stack([own, other], axis)
        return jnp.where(place == 0, straight, jnp.flip(straight, axis))

    one = ordered(pieces[0], pieces[1], places[second], 2)
    two = ordered(pieces[2], pieces[3], places[second], 2)
    whole = ordered(one, two, places[first], 1)
    if lead is None:
        return whole
    return jnp.take(whole, jnp.arange(extent[0]) ^ places[lead], axis=0)


def split_kernel(which, count, places, *refs):
    kept_ref, sent_ref = refs[count:]
    place = places[which]
    for ref, at in ((kept_ref, place), (sent_ref, 1 - place)):
        total = refs[0][:, at]
        if count > 1:
            total = total.astype(f32)
            for term in refs[1:count]:
                total = total + term[:, at].astype(f32)
        ref[...] = total.astype(bf16)


def split(places, which, parts, before):
    shape = parts[0].shape
    rest = shape[:before] + shape[before + 1 :]
    if shape[-2] % 16 == 0:
        flat = (math.prod(shape[:before]), 2, math.prod(shape[before + 1 : -1]), shape[-1])
        outs = [((flat[0],) + flat[2:], bf16)] * 2
        kernel = functools.partial(split_kernel, which, len(parts))
        halves = call(kernel, "split", outs, places, *[part.reshape(flat) for part in parts])
        return [half.reshape(rest) for half in halves]
    total = add(*parts)
    return [
        lax.dynamic_index_in_dim(total, at, before, False)
        for at in (places[which], 1 - places[which])
    ]


def halve(places, parts, steps):
    for name, which, before in steps:
        kept, sent = split(places, which, parts, before)
        parts = [kept, partner(sent, name)]
    return parts


def halves_swapped(values, half):
    lane = lax.broadcasted_iota(jnp.int32, values.shape, 1)
    up = pltpu.roll(values, half, 1)
    down = pltpu.roll(values, values.shape[1] - half, 1)
    return jnp.where(lane % (2 * half) < half, down, up)


def project_kernel(half, places, *refs):
    pieces, (weight_ref, cos_ref, sin_ref, q_ref, k_ref, v_ref) = refs[:8], refs[8:]
    width = q_ref.shape[1]
    rows = pieces[0].shape[0]
    for at in range(0, 8, 2):
        here = pl.ds(at * rows, 2 * rows)
        made = nn(jnp.concatenate([pieces[at][...], pieces[at + 1][...]]), weight_ref[...])
        cosine, sine = cos_ref[here, :], sin_ref[here, :]
        for place, ref in ((0, q_ref), (1, k_ref)):
            part = made[:, place * width : (place + 1) * width]
            ref[here, :] = (part * cosine + halves_swapped(part, half) * sine).astype(bf16)
        v_ref[here, :] = made[:, 2 * width :].astype(bf16)


def of_head(values, head, size):
    lane = lax.broadcasted_iota(jnp.int32, values.shape, 1)
    return jnp.where(lane // size == head, values, jnp.zeros_like(values))


def attend_kernel(size, places, q_ref, k_ref, v_ref, o_ref, log_ref):
    keys, values = k_ref[...], v_ref[...]
    block = o_ref.shape[1]
    step = log_ref.shape[2]
    scale = math.log2(math.e) / math.sqrt(size)

    def visit(i, carry):
        queries = q_ref[pl.ds(pl.multiple_of(i * step, step), step), :]
        outs = []
        for head in range(q_ref.shape[1] // size):
            scores = nt(keys, of_head(queries, head, size))
            top = jnp.max(scores, axis=0, keepdims=True)
            weights = jnp.exp2((scores - top) * scale)
            total = jnp.sum(weights, axis=0, keepdims=True)
            probs = (weights * (1.0 / total)).astype(bf16)
            outs.append(tn(values, probs)[head * size : (head + 1) * size])
            log_ref[i, head : head + 1, :] = top * scale + jnp.log2(total)
        out = jnp.transpose(jnp.concatenate(outs, axis=0)).astype(bf16)
        for at in range(step // block):
            chip = places[CHIP] ^ (i * (step // block) + at)
            o_ref[chip] = out[at * block : (at + 1) * block]
        return carry

    lax.fori_loop(0, q_ref.shape[0] // step, visit, 0)


def attend_back_kernel(
    size, together, places, q_ref, k_ref, v_ref, grad_ref, log_ref, cos_ref, sin_ref, dq_ref, dk_ref, dv_ref
):
    keys, values = k_ref[...], v_ref[...]
    block, width = grad_ref.shape[1:]
    step = log_ref.shape[2]
    scale = 1.0 / math.sqrt(size)
    exponent = scale * math.log2(math.e)
    dk_ref[...] = jnp.zeros_like(dk_ref)
    dv_ref[...] = jnp.zeros_like(dv_ref)

    def turned(part, here):
        back = halves_swapped(part, size // 2) * sin_ref[here, :]
        return (part * cos_ref[here, :] - back).astype(bf16)

    def visit(i, carry):
        here = pl.ds(pl.multiple_of(i * step, step), step)
        queries = q_ref[here, :]
        grads = [grad_ref[places[CHIP] ^ (i * (step // block) + at)] for at in range(step // block)]
        grads = jnp.concatenate(grads)
        outs = []
        for head in range(width // size):
            query, grad = of_head(queries, head, size), of_head(grads, head, size)
            probs = jnp.exp2(nt(keys, query) * exponent - log_ref[i, head : head + 1, :])
            grad_probs = nt(values, grad)
            delta = jnp.sum(probs * grad_probs, axis=0, keepdims=True)
            grad_scores = (probs * (grad_probs - delta)).astype(bf16)
            outs.append(tn(keys, grad_scores)[head * size : (head + 1) * size])
            dk_ref[...] += nn(grad_scores, query)
            dv_ref[...] += nn(probs.astype(bf16), grad)
        dq = jnp.transpose(jnp.concatenate(outs, axis=0)) * scale
        dq_ref[here, :width] = turned(dq, here)
        return carry

    lax.fori_loop(0, q_ref.shape[0] // step, visit, 0)
    if together:
        everything = pl.ds(0, q_ref.shape[0])
        dq_ref[:, width : 2 * width] = turned(dk_ref[...] * scale, everything)
        dq_ref[:, 2 * width :] = dv_ref[...].astype(bf16)
    else:
        dk_ref[...] = dk_ref[...] * scale


def turn_back_kernel(half, places, dq_ref, dk_ref, dv_ref, cos_ref, sin_ref, out_ref):
    width = dq_ref.shape[1]
    part = dk_ref[...]
    back = halves_swapped(part, half) * sin_ref[...]
    out_ref[:, :width] = dq_ref[...]
    out_ref[:, width : 2 * width] = (part * cos_ref[...] - back).astype(bf16)
    out_ref[:, 2 * width :] = dv_ref[...].astype(bf16)


def middle_kernel(places, arrived_ref, weight_ref, tokens_ref, attended_ref, middle_ref, low_ref):
    wide = arrived_ref.shape[2]
    for at in range(arrived_ref.shape[0]):
        attended_ref[:, at * wide : (at + 1) * wide] = arrived_ref[at]
    middle = tokens_ref[...].astype(f32) + nn(attended_ref[...], weight_ref[...])
    middle_ref[...] = middle
    low_ref[...] = normalize(middle)[0].astype(bf16)


def feed_kernel(places, *refs):
    two, cot, w_ref, (hidden_ref, grad_ref), outs = refs[:8], refs[8:16], refs[16], refs[17:19], refs[19:]
    piece = hidden_ref.shape[1]
    rows = two[0].shape[0]
    w_in, w_out = w_ref[:, : 2 * piece], w_ref[:, 2 * piece :]
    for at in (4, 6, 0, 2):
        here = pl.ds(at * rows, 2 * rows)
        gate_up = nn(jnp.concatenate([two[at][...], two[at + 1][...]]), w_in)
        grad_hidden = nn(jnp.concatenate([cot[at][...], cot[at + 1][...]]), w_out)
        gate, lift = gate_up[:, :piece], gate_up[:, piece:]
        cdf = 0.5 * (1.0 + lax.erf(gate * math.sqrt(0.5)))
        density = jnp.exp(-0.5 * gate * gate) * (1.0 / math.sqrt(2.0 * math.pi))
        activated = gate * cdf
        hidden_ref[here, :] = (activated * lift).astype(bf16)
        grad_gate = (grad_hidden * lift * (cdf + gate * density)).astype(bf16)
        grad_lift = (grad_hidden * activated).astype(bf16)
        grad_ref[here, :piece] = grad_gate
        grad_ref[here, piece:] = grad_lift
        made = nt(grad_gate, w_in[:, :piece]) + nt(grad_lift, w_in[:, piece:])
        made = made.astype(bf16)
        outs[at][...] = made[:rows]
        outs[at + 1][...] = made[rows:]


def feed(places, two, cot, weights):
    rows, width = two[0].shape
    piece = weights.shape[1] // 3
    outs = [((8 * rows, piece), bf16), ((8 * rows, 2 * piece), bf16)] + [((rows, width), bf16)] * 8
    hidden, grads, *terms = call(feed_kernel, "feed", outs, places, *two, *cot, weights, mib=24)
    return hidden, grads, terms


def feed_rest_kernel(places, *refs):
    two, cot, (hidden_ref, grad_ref, w_ref, out_ref), outs = refs[:8], refs[8:16], refs[16:20], refs[20:]
    piece = hidden_ref.shape[1]
    rows, width = two[0].shape
    w_out = w_ref[:, 2 * piece :]
    for at in (4, 6, 0, 2):
        made = nt(hidden_ref[pl.ds(at * rows, 2 * rows), :], w_out).astype(bf16)
        outs[at][...] = made[:rows]
        outs[at + 1][...] = made[rows:]
    step = width // 4
    for at in range(0, width, step):
        here = pl.ds(at, step)
        left = jnp.concatenate([ref[:, here] for ref in two])
        out_ref[here, : 2 * piece] = tn(left, grad_ref[...]).astype(bf16)
        left = jnp.concatenate([ref[:, here] for ref in cot])
        out_ref[here, 2 * piece :] = tn(left, hidden_ref[...]).astype(bf16)


def feed_rest(places, two, cot, hidden, grads, weights):
    rows, width = two[0].shape
    outs = [(weights.shape, bf16)] + [((rows, width), bf16)] * 8
    made, *terms = call(
        feed_rest_kernel, "feed_rest", outs, places, *two, *cot, hidden, grads, weights, mib=24
    )
    return made, terms


def result_kernel(places, middle_ref, a_ref, b_ref, c_ref, d_ref, e_ref, kept_ref, sent_ref):
    total = middle_ref[...]
    for ref in (a_ref, b_ref, c_ref, d_ref, e_ref):
        total = total + ref[...].astype(f32)
    total = total.astype(bf16)
    half = kept_ref.shape[0]
    kept_ref[...] = total[:half]
    sent_ref[...] = total[half:]


def middle_back_kernel(
    places, middle_ref, cot_ref, weight_ref, a_ref, b_ref, c_ref, d_ref, e_ref, grad_ref, low_ref, leaving_ref
):
    scaled = a_ref[...].astype(f32)
    for ref in (b_ref, c_ref, d_ref, e_ref):
        scaled = scaled + ref[...].astype(f32)
    normed, inverse = normalize(middle_ref[...])
    grad = cot_ref[...].astype(f32) + normalize_back(scaled, normed, inverse)
    grad_ref[...] = grad
    low = grad.astype(bf16)
    low_ref[...] = low
    made = nt(low, weight_ref[...]).astype(bf16)
    wide = leaving_ref.shape[2]
    for at in range(leaving_ref.shape[0]):
        leaving_ref[at] = made[:, at * wide : (at + 1) * wide]


def outer_kernel(places, left_ref, right_ref, out_ref):
    out_ref[...] = tn(left_ref[...], right_ref[...]).astype(bf16)


def project_back_kernel(places, grad_ref, weight_ref, *outs):
    rows = outs[0].shape[0]
    for at in (6, 4, 2, 0):
        made = nt(grad_ref[pl.ds(at * rows, 2 * rows), :], weight_ref[...]).astype(bf16)
        outs[at][...] = made[:rows]
        outs[at + 1][...] = made[rows:]


def project_outer_kernel(places, *refs):
    pieces, grad_ref, out_ref = refs[:8], refs[8], refs[9]
    width = pieces[0].shape[1]
    step = width // 4
    for at in range(0, width, step):
        left = jnp.concatenate([ref[:, pl.ds(at, step)] for ref in pieces])
        out_ref[pl.ds(at, step), :] = tn(left, grad_ref[...]).astype(bf16)


def tokens_back_kernel(places, tokens_ref, grad_ref, a_ref, b_ref, c_ref, d_ref, kept_ref, sent_ref):
    scaled = a_ref[...].astype(f32)
    for ref in (b_ref, c_ref, d_ref):
        scaled = scaled + ref[...].astype(f32)
    normed, inverse = normalize(tokens_ref[...].astype(f32))
    total = grad_ref[...] + normalize_back(scaled, normed, inverse)
    half = kept_ref.shape[0]
    kept_ref[...] = total[:half]
    sent_ref[...] = total[half:]


def columns_by(array, pieces, piece):
    rows, count = array.shape
    padded = jnp.pad(array, ((0, 0), (0, pieces * piece - count)))
    return jnp.swapaxes(padded.reshape(rows, pieces, piece), 0, 1)


def columns_back(array, count):
    pieces, rows, piece = array.shape
    return jnp.swapaxes(array, 0, 1).reshape(rows, pieces * piece)[:, :count]


def body(inputs, gain_attn, gain_mlp, w_qkv, w_attn_out, w_in, w_out, cotangent):
    pairs, squares = 8, 8
    rings = lax.axis_size("r")
    seqs, half_block, width = inputs.shape
    owned = w_qkv.shape[0]
    size = width // HEADS
    half = size // 2
    wide = width // pairs
    block = seqs * half_block
    span = pairs * block
    ff = w_out.shape[0]
    piece = -(-ff // (squares * LANES)) * LANES
    chips, square = ("zh", "zl", "x"), ("zl", "x", "c")
    ri, zh, zl, xi, ci, yi = (lax.axis_index(name) for name in ("r", "zh", "zl", "x", "c", "y"))
    places = jnp.stack([4 * zh + 2 * zl + xi, zh, zl, xi, ci, yi]).astype(jnp.int32)
    block_low, half_low = ((block, width), bf16), ((half_block, width), bf16)
    block_full, half_full = ((block, width), f32), ((half_block, width), f32)

    def over_rings(array):
        return lax.all_gather(array, "r", axis=0) if rings > 1 else array

    def ring_sums(array):
        if rings > 1:
            return lax.psum_scatter(array, "r", scatter_dimension=0, tiled=True)
        return array

    gain_one = gain_attn.astype(f32)[:, None]
    gain_two = gain_mlp.astype(f32)[:, None]

    tokens, low_one = call(
        enter_kernel, "enter", [block_low, block_low], places, inputs, partner(inputs, "c")
    )
    all_one = gather_chips(low_one)

    scaled_qkv = (w_qkv.astype(f32) * gain_one).astype(bf16)
    part = scaled_qkv.reshape(owned, 3, pairs, wide).transpose(2, 0, 1, 3)
    part = part.reshape(pairs, owned, 3 * wide)
    part = lax.all_to_all(part, chips, 0, 0, tiled=True)[:, None]
    part = [part, partner(part, "y")]
    part = part + [partner(member, "c") for member in part]
    pair_qkv = over_rings(assemble(places, None, C, Y, part)).reshape(width, 3 * wide)

    scaled_in = (w_in.astype(f32) * gain_two).astype(bf16)
    packed = jnp.concatenate(
        [
            columns_by(scaled_in[:, :ff], squares, piece),
            columns_by(scaled_in[:, ff:], squares, piece),
            columns_by(jnp.transpose(w_out), squares, piece),
        ],
        axis=2,
    )
    packed = lax.all_to_all(after(packed, low_one), square, 0, 0, tiled=True)[None]
    far = partner(packed, "zh")
    packed = [packed, partner(packed, "y"), far, partner(far, "y")]
    weights = over_rings(assemble(places, None, ZH, Y, packed)).reshape(width, 3 * piece)

    full = after(w_attn_out, low_one)
    full = jnp.stack([full, partner(full, "zh")])
    full = jnp.stack([full, partner(full, "zl")], axis=1)
    full = jnp.stack([full, partner(full, "x")], axis=2).reshape(8, 1, owned, width)
    full = [full, partner(full, "y")]
    full = full + [partner(member, "c") for member in full]
    full_attn = over_rings(assemble(places, CHIP, C, Y, full)).reshape(width, width)

    cotangent_here = call(
        pick_kernel, "pick", [block_low], places, cotangent, partner(cotangent, "c")
    )[0]
    all_cotangent = gather_square(after(cotangent_here, all_one[7]))

    chip_at = (places[CHIP] ^ jnp.arange(pairs, dtype=jnp.int32))[:, None, None]
    core_at = (ci ^ jnp.arange(2, dtype=jnp.int32))[None, :, None]
    at = jnp.arange(half_block, dtype=jnp.int32)[None, None, :]
    at = (ri * span + chip_at * block + core_at * half_block + at).reshape(span)
    frequency = rope_base ** (-2.0 * jnp.arange(half, dtype=jnp.int32).astype(f32) / size)
    angles = at.astype(f32)[:, None] * frequency[None, :]
    cosine = jnp.tile(jnp.cos(angles), (1, wide // half))
    sine = jnp.sin(angles)
    sine = jnp.tile(jnp.concatenate([-sine, sine], axis=1), (1, wide // size))
    queries, keys, values = call(
        functools.partial(project_kernel, half),
        "project",
        [((span, wide), bf16)] * 3,
        places,
        *all_one,
        pair_qkv,
        cosine,
        sine,
    )
    if rings > 1:
        keys = lax.all_gather(keys, "r", axis=0, tiled=True)
        values = lax.all_gather(values, "r", axis=0, tiled=True)
    count = keys.shape[0]
    step = 2 * block if count <= 2048 else block
    heads_out, logs = call(
        functools.partial(attend_kernel, size),
        "attend",
        [((pairs, block, wide), bf16), ((span // step, 8, step), f32)],
        places,
        queries,
        keys,
        values,
        mib=24,
    )
    arrived = lax.all_to_all(heads_out, chips, 0, 0, tiled=True)
    attended, middle, low_two = call(
        middle_kernel, "middle", [block_low, block_full, block_low], places, arrived, full_attn, tokens
    )
    all_two = gather_square(low_two)

    hidden, grad_gate_up, terms = feed(places, all_two, all_cotangent, weights)
    grad_two = scatter_square(terms)
    grad_weights, result = feed_rest(
        places, all_two, all_cotangent, hidden, grad_gate_up, weights
    )

    grad_middle, grad_branch, leaving = call(
        middle_back_kernel,
        "middle_back",
        [block_full, block_low, ((pairs, block, wide), bf16)],
        places,
        middle,
        cotangent_here,
        full_attn,
        *grad_two,
    )

    grad_heads = lax.all_to_all(leaving, chips, 0, 0, tiled=True)

    terms = ring_sums(grad_weights).reshape(2, squares, 2, owned, 3 * piece)
    terms = halve(places, [terms], [("y", Y, 2), ("zh", ZH, 0)])
    grad_packed = lax.all_to_all(add(*terms), square, 0, 0, tiled=True).astype(f32)
    grad_in = jnp.concatenate(
        [
            columns_back(grad_packed[:, :, :piece], ff),
            columns_back(grad_packed[:, :, piece : 2 * piece], ff),
        ],
        axis=1,
    )
    grad_out = jnp.transpose(columns_back(grad_packed[:, :, 2 * piece :], ff))
    grad_gain_mlp = jnp.sum(grad_in * w_in.astype(f32), axis=1)
    grad_in = grad_in * gain_two

    terms = call(outer_kernel, "outer", [((width, width), bf16)], places, attended, grad_branch)[0]
    terms = ring_sums(terms).reshape(2, 2, 2, 2, 2, owned, width)
    steps = [("c", C, 3), ("y", Y, 3), ("x", X, 2), ("zl", ZL, 1), ("zh", ZH, 0)]
    kept, sent = halve(places, [terms], steps)
    grad_attn = kept.astype(f32) + sent.astype(f32)

    result = [after(result[0], grad_heads)] + result[1:]
    kept, sent = call(
        result_kernel, "result", [half_low] * 2, places, middle, *scatter_square(result)
    )
    output = call(
        leave_kernel, "leave", [(inputs.shape, bf16)], places, kept, partner(sent, "c")
    )[0]

    parts = [queries, keys, values, grad_heads, logs, cosine, sine]
    kernel = functools.partial(attend_back_kernel, size, rings == 1)
    if rings == 1:
        grad_projected = call(
            kernel,
            "attend_back",
            [((span, 3 * wide), bf16)],
            places,
            *parts,
            scratch=[pltpu.VMEM((count, wide), f32)] * 2,
            mib=24,
        )[0]
    else:
        outs = [((span, wide), bf16), ((count, wide), f32), ((count, wide), f32)]
        grad_q, grad_k, grad_v = call(kernel, "attend_back", outs, places, *parts, mib=36)
        grad_projected = call(
            functools.partial(turn_back_kernel, half),
            "turn_back",
            [((span, 3 * wide), bf16)],
            places,
            grad_q,
            ring_sums(grad_k),
            ring_sums(grad_v),
            cosine,
            sine,
        )[0]

    terms = call(
        project_back_kernel, "project_back", [block_low] * 8, places, grad_projected, pair_qkv
    )
    kept, sent = call(
        tokens_back_kernel,
        "tokens_back",
        [half_full] * 2,
        places,
        tokens,
        grad_middle,
        *scatter_chips(terms),
    )
    input_grad = call(
        leave_kernel, "leave", [(inputs.shape, f32)], places, kept, partner(sent, "c")
    )[0]

    terms = call(
        project_outer_kernel,
        "project_outer",
        [((width, 3 * wide), bf16)],
        places,
        *all_one,
        grad_projected,
    )[0]
    terms = ring_sums(terms).reshape(pairs, 2, 2, owned, 3 * wide)
    terms = halve(places, [terms], [("c", C, 1), ("y", Y, 1)])
    terms = lax.all_to_all(add(*terms), chips, 0, 0, tiled=True).astype(f32)
    grad_qkv = terms.reshape(pairs, owned, 3, wide).transpose(1, 2, 0, 3).reshape(owned, 3 * width)
    grad_gain_attn = jnp.sum(grad_qkv * w_qkv.astype(f32), axis=1)
    grad_qkv = grad_qkv * gain_one
    return (
        output,
        input_grad,
        grad_gain_attn,
        grad_gain_mlp,
        grad_qkv,
        grad_attn,
        grad_in,
        grad_out,
    )


def solution(mesh):
    ctx, fsdp = mesh.shape["ctx"], mesh.shape["fsdp"]
    everyone = ("r", "zh", "zl", "x", "c", "y")
    grid = Mesh(mesh.devices.reshape(ctx // 16, 2, 2, 2, 2, fsdp), everyone)
    tokens = P("y", everyone[:-1], None)
    gain, rows, columns = P(everyone), P(everyone, None), P(None, everyone)
    return jax.shard_map(
        body,
        mesh=grid,
        in_specs=(tokens, gain, gain, rows, rows, rows, columns, tokens),
        out_specs=(tokens, tokens, gain, gain, rows, rows, rows, columns),
        check_vma=False,
    )
```

```python
import functools
import math

import jax
import jax.numpy as jnp
from jax import lax
from jax.experimental import pallas as pl
from jax.experimental.pallas import tpu as pltpu
from jax.sharding import Mesh
from jax.sharding import PartitionSpec as P

HEADS = 16
norm_eps = 1e-05
rope_base = 160000.0
f32 = jnp.float32
bf16 = jnp.bfloat16
LANES = 128
MIB = 1024 * 1024


def partner(array, axis):
    return lax.ppermute(array, axis, [(0, 1), (1, 0)])


def opposite(array, axes):
    return lax.ppermute(array, axes, [(i, 3 - i) for i in range(4)])


def after(array, *others):
    return lax.optimization_barrier((array, *others))[0]


def fence(live):
    return dict(zip(live, lax.optimization_barrier(tuple(live.values()))))


def add(*terms):
    total = terms[0].astype(f32)
    for term in terms[1:]:
        total = total + term.astype(f32)
    return total.astype(terms[0].dtype)


def call(kernel, name, outs, places, *arrays, scratch=(), mib=16, flops=0, exps=0):
    vmem = pl.BlockSpec(memory_space=pltpu.VMEM)
    moved = sum(array.size * array.dtype.itemsize for array in arrays)
    moved += sum(math.prod(shape) * jnp.dtype(dtype).itemsize for shape, dtype in outs)
    return pl.pallas_call(
        kernel,
        in_specs=[pl.BlockSpec(memory_space=pltpu.SMEM)] + [vmem] * len(arrays),
        out_specs=[vmem] * len(outs),
        out_shape=[jax.ShapeDtypeStruct(shape, dtype) for shape, dtype in outs],
        scratch_shapes=list(scratch),
        compiler_params=pltpu.CompilerParams(vmem_limit_bytes=mib * MIB),
        cost_estimate=pl.CostEstimate(flops=flops, bytes_accessed=moved, transcendentals=exps),
        name=name,
    )(places, *arrays)


CHIP, ZH, ZL, X, C, Y = range(6)


def nt(left, right):
    return lax.dot_general(left, right, (((1,), (1,)), ((), ())), preferred_element_type=f32)


def tn(left, right):
    return lax.dot_general(left, right, (((0,), (0,)), ((), ())), preferred_element_type=f32)


def nn(left, right):
    return lax.dot_general(left, right, (((1,), (0,)), ((), ())), preferred_element_type=f32)


def normalize(values):
    centre = values - jnp.mean(values, axis=-1, keepdims=True)
    inverse = lax.rsqrt(jnp.mean(centre * centre, axis=-1, keepdims=True) + norm_eps)
    return centre * inverse, inverse


def normalize_back(scaled, normed, inverse):
    inner = jnp.mean(scaled * normed, axis=-1, keepdims=True)
    return inverse * (scaled - jnp.mean(scaled, axis=-1, keepdims=True) - normed * inner)


def pick_kernel(places, own_ref, other_ref, block_ref):
    half = own_ref.shape[1]
    block_ref[:half, :] = own_ref[places[C]]
    block_ref[half:, :] = other_ref[places[C]]


def enter_kernel(places, own_ref, other_ref, cot_a_ref, cot_b_ref, block_ref, cot_ref, low_ref):
    pick_kernel(places, own_ref, other_ref, block_ref)
    pick_kernel(places, cot_a_ref, cot_b_ref, cot_ref)
    low_ref[...] = normalize(block_ref[...].astype(f32))[0].astype(bf16)


def leave_kernel(places, own_ref, other_ref, out_ref):
    out_ref[places[C]] = own_ref[...]
    out_ref[1 - places[C]] = other_ref[...]


def assemble_kernel(lead, first, second, places, a_ref, b_ref, c_ref, d_ref, out_ref):
    chip = places[lead] if lead is not None else 0
    one, two = places[first], places[second]
    for i, row in enumerate(((a_ref, b_ref), (c_ref, d_ref))):
        for j, ref in enumerate(row):
            for at in range(ref.shape[0]):
                out_ref[chip ^ at, one ^ i, :, two ^ j] = ref[at]


def assemble(places, lead, first, second, pieces):
    extent = pieces[0].shape
    shape = (extent[0], 2, extent[1], 2) + extent[2:]
    if extent[2] % 16 == 0:
        kernel = functools.partial(assemble_kernel, lead, first, second)
        return call(kernel, "assemble", [(shape, bf16)], places, *pieces)[0]

    def ordered(own, other, place, axis):
        straight = jnp.stack([own, other], axis)
        return jnp.where(place == 0, straight, jnp.flip(straight, axis))

    one = ordered(pieces[0], pieces[1], places[second], 2)
    two = ordered(pieces[2], pieces[3], places[second], 2)
    whole = ordered(one, two, places[first], 1)
    if lead is None:
        return whole
    return jnp.take(whole, jnp.arange(extent[0]) ^ places[lead], axis=0)


def assemble_rows_kernel(places, a_ref, b_ref, c_ref, d_ref, out_ref):
    for i, row in enumerate(((a_ref, b_ref), (c_ref, d_ref))):
        for j, ref in enumerate(row):
            for at in range(4):
                for k in range(2):
                    out_ref[places[CHIP] ^ (2 * at + j), places[C] ^ i, places[Y] ^ k] = ref[at, k]


def assemble_rows(places, pieces):
    if pieces[0].shape[2] % 16 == 0:
        shape = (8, 2) + pieces[0].shape[1:]
        return call(assemble_rows_kernel, "assemble_rows", [(shape, bf16)], places, *pieces)[0]
    merged = [jnp.stack(pieces[at : at + 2], axis=1) for at in (0, 2)]
    merged = [member.reshape((8, 1) + member.shape[2:]) for member in merged]
    pieces = [member[:, :, at] for member in merged for at in range(2)]
    return assemble(places, CHIP, C, Y, pieces)


def total_kernel(places, a_ref, b_ref, out_ref):
    out_ref[...] = (a_ref[...].astype(f32) + b_ref[...].astype(f32)).astype(bf16)


def total(places, kept, other):
    if kept.shape[1] % 16 == 0:
        return call(total_kernel, "total", [(kept.shape, bf16)], places, kept, other)[0]
    return add(kept, other)


def put_shares(made, place, at, kept_ref, sent_ref):
    share, width = kept_ref.shape[1:]
    groups = made.shape[0] // (2 * share)
    made = made.reshape(groups, 2, share, width)
    kept_ref[pl.ds(at, groups)] = jnp.where(place == 0, made[:, 0], made[:, 1]).astype(bf16)
    sent_ref[pl.ds(at, groups)] = jnp.where(place == 0, made[:, 1], made[:, 0]).astype(bf16)


def split_kernel(which, count, places, *refs):
    kept_ref, sent_ref = refs[count:]
    place = places[which]
    for ref, at in ((kept_ref, place), (sent_ref, 1 - place)):
        total = refs[0][:, at]
        if count > 1:
            total = total.astype(f32)
            for term in refs[1:count]:
                total = total + term[:, at].astype(f32)
        ref[...] = total.astype(bf16)


def split(places, which, parts, before):
    shape = parts[0].shape
    rest = shape[:before] + shape[before + 1 :]
    if shape[-2] % 16 == 0:
        flat = (math.prod(shape[:before]), 2, math.prod(shape[before + 1 : -1]), shape[-1])
        outs = [((flat[0],) + flat[2:], bf16)] * 2
        kernel = functools.partial(split_kernel, which, len(parts))
        halves = call(kernel, "split", outs, places, *[part.reshape(flat) for part in parts])
        return [half.reshape(rest) for half in halves]
    total = add(*parts)
    return [
        lax.dynamic_index_in_dim(total, at, before, False)
        for at in (places[which], 1 - places[which])
    ]


def halves_swapped(values, half):
    lane = lax.broadcasted_iota(jnp.int32, values.shape, 1)
    up = pltpu.roll(values, half, 1)
    down = pltpu.roll(values, values.shape[1] - half, 1)
    return jnp.where(lane % (2 * half) < half, down, up)


def project_kernel(half, places, *refs):
    pieces, (weight_ref, table_ref, out_ref, stack_ref) = refs[:8], refs[8:]
    width = out_ref.shape[1] // 3
    rows = pieces[0].shape[0]
    for at in range(0, 8, 2):
        here = pl.ds(at * rows, 2 * rows)
        both = jnp.concatenate([ref[...] for ref in pieces[at : at + 2]])
        stack_ref[here, :] = both
        made = nn(both, weight_ref[...])
        cosine, sine = table_ref[here, :width], table_ref[here, width:]
        for place in range(2):
            part = made[:, place * width : (place + 1) * width]
            turned = part * cosine + halves_swapped(part, half) * sine
            out_ref[here, place * width : (place + 1) * width] = turned.astype(bf16)
        out_ref[here, 2 * width :] = made[:, 2 * width :].astype(bf16)


def of_head(values, head, size):
    lane = lax.broadcasted_iota(jnp.int32, values.shape, 1)
    return jnp.where(lane // size == head, values, jnp.zeros_like(values))


def keys_and_values(refs, width):
    if len(refs) == 1:
        return refs[0][:, width : 2 * width], refs[0][:, 2 * width :]
    return refs[1][:, :width], refs[1][:, width:]


def attend_kernel(size, places, *refs):
    refs, (o_ref, log_ref) = refs[:-2], refs[-2:]
    block, width = o_ref.shape[1:]
    keys, values = keys_and_values(refs, width)
    step = log_ref.shape[2]
    scale = math.log2(math.e) / math.sqrt(size)

    def visit(i, carry):
        queries = refs[0][pl.ds(pl.multiple_of(i * step, step), step), :width]
        outs = []
        for head in range(width // size):
            scores = nt(keys, of_head(queries, head, size))
            top = jnp.max(scores, axis=0, keepdims=True)
            weights = jnp.exp2((scores - top) * scale)
            total = jnp.sum(weights, axis=0, keepdims=True)
            probs = (weights * (1.0 / total)).astype(bf16)
            outs.append(tn(values, probs)[head * size : (head + 1) * size])
            log_ref[i, head : head + 1, :] = top * scale + jnp.log2(total)
        out = jnp.transpose(jnp.concatenate(outs, axis=0)).astype(bf16)
        for at in range(step // block):
            chip = places[CHIP] ^ (i * (step // block) + at)
            o_ref[chip] = out[at * block : (at + 1) * block]
        return carry

    lax.fori_loop(0, refs[0].shape[0] // step, visit, 0)


def attend_back_kernel(size, together, places, *refs):
    refs, (grad_ref, log_ref, table_ref, dq_ref, dk_ref, dv_ref) = refs[:-6], refs[-6:]
    block, width = grad_ref.shape[1:]
    keys, values = keys_and_values(refs, width)
    step = log_ref.shape[2]
    scale = 1.0 / math.sqrt(size)
    exponent = scale * math.log2(math.e)
    dk_ref[...] = jnp.zeros_like(dk_ref)
    dv_ref[...] = jnp.zeros_like(dv_ref)

    def turned(part, here):
        back = halves_swapped(part, size // 2) * table_ref[here, width:]
        return (part * table_ref[here, :width] - back).astype(bf16)

    def visit(i, carry):
        here = pl.ds(pl.multiple_of(i * step, step), step)
        queries = refs[0][here, :width]
        grads = [grad_ref[places[CHIP] ^ (i * (step // block) + at)] for at in range(step // block)]
        grads = jnp.concatenate(grads)
        outs = []
        for head in range(width // size):
            query, grad = of_head(queries, head, size), of_head(grads, head, size)
            probs = jnp.exp2(nt(keys, query) * exponent - log_ref[i, head : head + 1, :])
            grad_probs = nt(values, grad)
            delta = jnp.sum(probs * grad_probs, axis=0, keepdims=True)
            grad_scores = (probs * (grad_probs - delta)).astype(bf16)
            outs.append(tn(keys, grad_scores)[head * size : (head + 1) * size])
            dk_ref[...] += nn(grad_scores, query)
            dv_ref[...] += nn(probs.astype(bf16), grad)
        dq = jnp.transpose(jnp.concatenate(outs, axis=0)) * scale
        dq_ref[here, :width] = turned(dq, here)
        return carry

    lax.fori_loop(0, refs[0].shape[0] // step, visit, 0)
    if together:
        everything = pl.ds(0, dq_ref.shape[0])
        dq_ref[:, width : 2 * width] = turned(dk_ref[...] * scale, everything)
        dq_ref[:, 2 * width :] = dv_ref[...].astype(bf16)
    else:
        dk_ref[...] = dk_ref[...] * scale


def turn_back_kernel(half, places, dq_ref, dk_ref, dv_ref, table_ref, out_ref):
    width = dq_ref.shape[1]
    part = dk_ref[...]
    back = halves_swapped(part, half) * table_ref[:, width:]
    out_ref[:, :width] = dq_ref[...]
    out_ref[:, width : 2 * width] = (part * table_ref[:, :width] - back).astype(bf16)
    out_ref[:, 2 * width :] = dv_ref[...].astype(bf16)


def middle_kernel(places, arrived_ref, weight_ref, tokens_ref, attended_ref, middle_ref, low_ref):
    wide = arrived_ref.shape[2]
    for at in range(arrived_ref.shape[0]):
        attended_ref[:, at * wide : (at + 1) * wide] = arrived_ref[at]
    middle = tokens_ref[...].astype(f32) + nn(attended_ref[...], weight_ref[...])
    middle_ref[...] = middle
    low_ref[...] = normalize(middle)[0].astype(bf16)


def feed_kernel(places, *refs):
    two, cot, (w_ref, hidden_ref, grad_ref), outs = refs[:8], refs[8:16], refs[16:19], refs[19:]
    piece = hidden_ref.shape[1]
    rows = two[0].shape[0]
    w_in, w_out = w_ref[:, : 2 * piece], w_ref[:, 2 * piece :]
    for at in (4, 6, 0, 2):
        here = pl.ds(at * rows, 2 * rows)
        gate_up = nn(jnp.concatenate([two[at][...], two[at + 1][...]]), w_in)
        grad_hidden = nn(jnp.concatenate([cot[at][...], cot[at + 1][...]]), w_out)
        gate, lift = gate_up[:, :piece], gate_up[:, piece:]
        cdf = 0.5 * (1.0 + lax.erf(gate * math.sqrt(0.5)))
        density = jnp.exp(-0.5 * gate * gate) * (1.0 / math.sqrt(2.0 * math.pi))
        activated = gate * cdf
        hidden_ref[here, :] = (activated * lift).astype(bf16)
        grad_gate = (grad_hidden * lift * (cdf + gate * density)).astype(bf16)
        grad_lift = (grad_hidden * activated).astype(bf16)
        grad_ref[here, :piece] = grad_gate
        grad_ref[here, piece:] = grad_lift
        made = nt(grad_gate, w_in[:, :piece]) + nt(grad_lift, w_in[:, piece:])
        outs[at // 4][pl.ds(at % 4 * rows, 2 * rows), :] = made.astype(bf16)


def feed(places, two, cot, weights):
    rows, width = two[0].shape
    piece = weights.shape[1] // 3
    outs = [((8 * rows, piece), bf16), ((8 * rows, 2 * piece), bf16)] + [((4 * rows, width), bf16)] * 2
    hidden, grads, *terms = call(
        feed_kernel,
        "feed",
        outs,
        places,
        *two,
        *cot,
        weights,
        mib=24,
        flops=80 * rows * width * piece,
        exps=16 * rows * piece,
    )
    return hidden, grads, terms


def feed_rest_kernel(places, *refs):
    two, cot, (hidden_ref, grad_ref, w_ref), outs, made_refs = (
        refs[:8],
        refs[8:16],
        refs[16:19],
        refs[19:21],
        refs[21:],
    )
    piece = hidden_ref.shape[1]
    rows, width = two[0].shape
    w_out = w_ref[:, 2 * piece :]
    for at in (4, 6, 0, 2):
        made = nt(hidden_ref[pl.ds(at * rows, 2 * rows), :], w_out)
        outs[at // 4][pl.ds(at % 4 * rows, 2 * rows), :] = made.astype(bf16)
    step = width // 4
    for at in range(0, width, step):
        here = pl.ds(at, step)
        left = jnp.concatenate([ref[:, here] for ref in two])
        made = tn(left, grad_ref[...])
        left = jnp.concatenate([ref[:, here] for ref in cot])
        made = jnp.concatenate([made, tn(left, hidden_ref[...])], axis=1)
        if len(made_refs) == 1:
            made_refs[0][here, :] = made.astype(bf16)
        else:
            put_shares(made, places[Y], at // (2 * made_refs[0].shape[1]), *made_refs)


def feed_rest(places, two, cot, hidden, grads, weights, shares):
    rows, width = two[0].shape
    outs = [((4 * rows, width), bf16)] * 2 + [(shape, bf16) for shape in shares]
    made = call(
        feed_rest_kernel,
        "feed_rest",
        outs,
        places,
        *two,
        *cot,
        hidden,
        grads,
        weights,
        mib=24,
        flops=64 * rows * width * (weights.shape[1] // 3),
    )
    return made[:2], made[2:]


def chip_sums_kernel(places, a_ref, b_ref, *outs):
    rows = outs[0].shape[0]
    for at, ref in enumerate(outs):
        here = pl.ds(at * rows, rows)
        ref[...] = (a_ref[here, :].astype(f32) + b_ref[here, :].astype(f32)).astype(bf16)


def chip_sums(places, here, there):
    shape = (here.shape[0] // 4, here.shape[1])
    return call(chip_sums_kernel, "chip_sums", [(shape, bf16)] * 4, places, here, partner(there, "c"))


def far_sums_kernel(places, kept_ref, across_ref, six_ref, four_ref):
    rows = six_ref.shape[0]
    for at, ref in enumerate((six_ref, four_ref)):
        here = pl.ds(at * rows, rows)
        ref[...] = (kept_ref[here, :].astype(f32) + across_ref[here, :].astype(f32)).astype(bf16)


def near_sums_kernel(places, kept_ref, across_ref, four_ref, both_ref, two_ref, own_ref, out_ref):
    far_sums_kernel(places, kept_ref, across_ref, two_ref, own_ref)
    out_ref[...] = (four_ref[...].astype(f32) + both_ref[...].astype(f32)).astype(bf16)


def result_kernel(places, middle_ref, a_ref, b_ref, c_ref, d_ref, kept_ref, sent_ref):
    total = middle_ref[...]
    for ref in (a_ref, b_ref, c_ref, d_ref):
        total = total + ref[...].astype(f32)
    total = total.astype(bf16)
    half = kept_ref.shape[0]
    kept_ref[...] = total[:half]
    sent_ref[...] = total[half:]


def middle_back_kernel(
    places, middle_ref, cot_ref, weight_ref, a_ref, b_ref, c_ref, d_ref, grad_ref, low_ref, leaving_ref
):
    scaled = a_ref[...].astype(f32)
    for ref in (b_ref, c_ref, d_ref):
        scaled = scaled + ref[...].astype(f32)
    normed, inverse = normalize(middle_ref[...])
    grad = cot_ref[...].astype(f32) + normalize_back(scaled, normed, inverse)
    grad_ref[...] = grad
    low = grad.astype(bf16)
    low_ref[...] = low
    made = nt(low, weight_ref[...]).astype(bf16)
    wide = leaving_ref.shape[2]
    for at in range(leaving_ref.shape[0]):
        leaving_ref[at] = made[:, at * wide : (at + 1) * wide]


def outer_kernel(places, left_ref, right_ref, *made_refs):
    made = tn(left_ref[...], right_ref[...])
    if len(made_refs) == 1:
        made_refs[0][...] = made.astype(bf16)
    else:
        put_shares(made, places[C], 0, *made_refs)


def project_back_kernel(places, grad_ref, weight_ref, *outs):
    rows = outs[0].shape[0] // 2
    for at in (6, 4, 2, 0):
        made = nt(grad_ref[pl.ds(at * rows, 2 * rows), :], weight_ref[...]).astype(bf16)
        first = 0 if at >= 4 else 2
        here = pl.ds((0 if at in (6, 2) else 1) * rows, rows)
        outs[first][here, :] = made[:rows]
        outs[first + 1][here, :] = made[rows:]


def project_outer_kernel(places, left_ref, grad_ref, *made_refs):
    width = left_ref.shape[1]
    step = width // 4
    for at in range(0, width, step):
        made = tn(left_ref[:, pl.ds(at, step)], grad_ref[...])
        if len(made_refs) == 1:
            made_refs[0][pl.ds(at, step), :] = made.astype(bf16)
        else:
            put_shares(made, places[C], at // (2 * made_refs[0].shape[1]), *made_refs)


def tokens_back_kernel(places, tokens_ref, grad_ref, a_ref, b_ref, c_ref, kept_ref, sent_ref):
    scaled = a_ref[...].astype(f32)
    for ref in (b_ref, c_ref):
        scaled = scaled + ref[...].astype(f32)
    normed, inverse = normalize(tokens_ref[...].astype(f32))
    total = grad_ref[...] + normalize_back(scaled, normed, inverse)
    half = kept_ref.shape[0]
    kept_ref[...] = total[:half]
    sent_ref[...] = total[half:]


def columns_by(array, pieces, piece):
    rows, count = array.shape
    padded = jnp.pad(array, ((0, 0), (0, pieces * piece - count)))
    return jnp.swapaxes(padded.reshape(rows, pieces, piece), 0, 1)


def columns_back(array, count):
    pieces, rows, piece = array.shape
    return jnp.swapaxes(array, 0, 1).reshape(rows, pieces * piece)[:, :count]


def body(inputs, gain_attn, gain_mlp, w_qkv, w_attn_out, w_in, w_out, cotangent):
    pairs, squares = 8, 8
    rings = lax.axis_size("r")
    seqs, half_block, width = inputs.shape
    owned = w_qkv.shape[0]
    size = width // HEADS
    half = size // 2
    wide = width // pairs
    block = seqs * half_block
    span = pairs * block
    ff = w_out.shape[0]
    piece = -(-ff // (squares * LANES)) * LANES
    chips, square = ("zh", "zl", "x"), ("zl", "x", "c")
    ri, zh, zl, xi, ci, yi = (lax.axis_index(name) for name in ("r", "zh", "zl", "x", "c", "y"))
    places = jnp.stack([4 * zh + 2 * zl + xi, zh, zl, xi, ci, yi]).astype(jnp.int32)
    block_low, half_low = ((block, width), bf16), ((half_block, width), bf16)
    block_full, half_full = ((block, width), f32), ((half_block, width), f32)

    def over_rings(array):
        return lax.all_gather(array, "r", axis=0) if rings > 1 else array

    def ring_sums(array):
        if rings > 1:
            return lax.psum_scatter(array, "r", scatter_dimension=0, tiled=True)
        return array

    gain_one = gain_attn.astype(f32)[:, None]
    gain_two = gain_mlp.astype(f32)[:, None]


    tokens, cot, low_one = call(
        enter_kernel,
        "enter",
        [block_low] * 3,
        places,
        inputs,
        partner(inputs, "c"),
        cotangent,
        partner(cotangent, "c"),
    )
    scaled_qkv = (w_qkv.astype(f32) * gain_one).astype(bf16)
    slices = scaled_qkv.reshape(owned, 3, pairs, wide).transpose(2, 0, 1, 3)
    live = {"tokens": tokens, "cot": cot, "one0": low_one}
    live |= {"slices": slices.reshape(pairs, owned, 3 * wide), "attn": w_attn_out}
    live |= {"in": w_in, "out": w_out, "places": places}
    live = fence(live)

    one4 = partner(live["one0"], "zh")
    one2 = partner(live["one0"], "zl")
    one1 = partner(live["one0"], "x")
    cot_x = partner(live["cot"], "x")
    qkv = lax.all_to_all(live.pop("slices"), chips, 0, 0, tiled=True)[:, None]
    full = live.pop("attn")
    full = jnp.stack([full, partner(full, "y")])
    scaled_in = (live.pop("in").astype(f32) * gain_two).astype(bf16)
    packed = jnp.concatenate(
        [
            columns_by(scaled_in[:, :ff], squares, piece),
            columns_by(scaled_in[:, ff:], squares, piece),
            columns_by(jnp.transpose(live.pop("out")), squares, piece),
        ],
        axis=2,
    )
    live |= {"one1": one1, "one2": one2, "one4": one4, "full": full, "packed": packed}
    live["cot_x"] = cot_x
    live = fence(live)

    places = live["places"]
    one6 = partner(live["one4"], "zl")
    one5 = partner(live["one4"], "x")
    one3 = partner(live["one2"], "x")
    packed = lax.all_to_all(live.pop("packed"), square, 0, 0, tiled=True)[None]
    full = live.pop("full")
    full = jnp.stack([full, partner(full, "zh")])
    lane = jnp.arange(wide, dtype=jnp.int32)
    frequency = rope_base ** (-2.0 * (lane % half).astype(f32) / size)
    sign = jnp.where(lane % size < half, -1.0, 1.0)
    row = jnp.arange(span, dtype=jnp.int32)
    at = (places[CHIP] ^ (row // block)) * block + (places[C] ^ (row % block // half_block)) * half_block
    at = ri * span + at + row % half_block
    angles = at.astype(f32)[:, None] * frequency[None, :]
    table = jnp.concatenate([jnp.cos(angles), jnp.sin(angles) * sign], axis=1)
    live |= {"one3": one3, "one5": one5, "one6": one6, "qkv": qkv, "table": table, "full": full}
    live["packed"] = packed
    live = fence(live)

    one7 = partner(live["one6"], "x")
    qkv = live.pop("qkv")
    qkv = [qkv, partner(qkv, "y")]
    qkv = qkv + [partner(member, "c") for member in qkv]
    cot_z = partner(live["cot"], "zl")
    full = live.pop("full")
    full = jnp.stack([full, partner(full, "zl")], axis=1)
    pair_qkv = over_rings(assemble(places, None, C, Y, qkv)).reshape(width, 3 * wide)
    live |= {"one7": one7, "qkv": pair_qkv, "full": full}
    live = fence(live)

    full_x = partner(live["full"], "x")
    packed_far = partner(live["packed"], "zh")
    packed_y = partner(live["packed"], "y")
    projected, all_one = call(
        functools.partial(project_kernel, half),
        "project",
        [((span, 3 * wide), bf16), ((span, width), bf16)],
        places,
        *[live.pop(f"one{j}") for j in range(8)],
        live["qkv"],
        live["table"],
        flops=6 * span * width * wide,
    )
    projected = [projected]
    if rings > 1:
        projected += [lax.all_gather(projected[0][:, wide:], "r", axis=0, tiled=True)]
    count = projected[-1].shape[0]
    step = 2 * block if count <= 2048 else block
    heads_out, logs = call(
        functools.partial(attend_kernel, size),
        "attend",
        [((pairs, block, wide), bf16), ((span // step, 8, step), f32)],
        places,
        *projected,
        mib=24,
        flops=16 * span * count * wide,
        exps=2 * span * count,
    )
    live |= {"heads": heads_out, "full_x": full_x, "cot_z": cot_z}
    live = fence(live)

    arrived = lax.all_to_all(live.pop("heads"), chips, 0, 0, tiled=True)
    cot_zx = partner(live["cot_z"], "x")
    full = [member.reshape(4, 2, owned, width) for member in (live.pop("full"), live.pop("full_x"))]
    full = full + [partner(member, "c") for member in full]
    full_attn = over_rings(assemble_rows(places, full)).reshape(width, width)
    live |= {"arrived": arrived, "attn": full_attn}
    live |= {"far": packed_far, "packed_y": packed_y, "cot_zx": cot_zx}
    live = fence(live)

    far_y = partner(live["far"], "y")
    attended, middle, low_two = call(
        middle_kernel,
        "middle",
        [block_low, block_full, block_low],
        places,
        live.pop("arrived"),
        live["attn"],
        live["tokens"],
        flops=2 * block * width * width,
    )
    live |= {"attended": attended, "middle": middle, "two": low_two}
    live = fence(live)

    over_x = partner(live["two"], "x")
    over_z = partner(live["two"], "zl")
    over_both = opposite(live["two"], ("zl", "x"))
    all_cotangent = [live[name] for name in ("cot", "cot_x", "cot_z", "cot_zx")]
    all_cotangent += [partner(member, "c") for member in all_cotangent]
    packed = [live.pop("packed"), live.pop("packed_y"), live.pop("far"), far_y]
    weights = assemble(places, None, ZH, Y, packed)
    live["weights"] = over_rings(weights).reshape(width, 3 * piece)
    live |= {"over_x": over_x, "over_z": over_z, "over_both": over_both}
    live = fence(live)

    all_two = [live.pop(name) for name in ("two", "over_x", "over_z", "over_both")]
    all_two += [partner(member, "c") for member in all_two]
    hidden, grad_gate_up, terms = feed(places, all_two, all_cotangent, live["weights"])
    live |= {"hidden": hidden, "gate_up": grad_gate_up}
    live |= {"here": terms[0], "there": terms[1]}
    live = fence(live)

    sums = chip_sums(places, live.pop("here"), live.pop("there"))
    live |= {f"sum{j}": member for j, member in enumerate(sums)}
    live = fence(live)

    sums = [live.pop(f"sum{j}") for j in range(4)]
    over_both = opposite(sums[3], ("zl", "x"))
    over_x = partner(sums[1], "x")
    over_z = partner(sums[2], "zl")
    direct = rings == 1 and owned % 16 == 0
    shape = (2 * squares, owned, 3 * piece)
    result, shares = feed_rest(
        places,
        all_two,
        all_cotangent,
        live.pop("hidden"),
        live.pop("gate_up"),
        live.pop("weights"),
        [shape] * 2 if direct else [(width, 3 * piece)],
    )
    if not direct:
        terms = ring_sums(shares[0]).reshape(2 * squares, 2, owned, 3 * piece)
        shares = split(places, Y, [terms], 1)
    weights_kept, weights_y = shares[0], partner(shares[1], "y")
    live |= {"result_here": result[0], "result_there": result[1]}
    live |= {f"sum{j}": m for j, m in enumerate([sums[0], over_x, over_z, over_both])}
    live["weights_kept"] = weights_kept
    live = fence(live)

    grad_middle, grad_branch, leaving = call(
        middle_back_kernel,
        "middle_back",
        [block_full, block_low, ((pairs, block, wide), bf16)],
        places,
        live["middle"],
        live.pop("cot"),
        live.pop("attn"),
        *[live.pop(f"sum{j}") for j in range(4)],
        flops=2 * block * width * width,
    )
    live |= {"grad_middle": grad_middle, "branch": grad_branch, "leaving": leaving}
    live = fence(live)

    grad_heads = lax.all_to_all(live.pop("leaving"), chips, 0, 0, tiled=True)
    result = chip_sums(places, live.pop("result_here"), live.pop("result_there"))
    result_both = opposite(result[3], ("zl", "x"))
    result_x = partner(result[1], "x")
    result_z = partner(result[2], "zl")
    live["result0"] = result[0]
    shape = (pairs, 2 * owned, width)
    shares = call(
        outer_kernel,
        "outer",
        [(shape, bf16)] * 2 if direct else [((width, width), bf16)],
        places,
        live.pop("attended"),
        live.pop("branch"),
        flops=2 * block * width * width,
    )
    if not direct:
        shares = split(places, C, [ring_sums(shares[0]).reshape(pairs, 2, 2 * owned, width)], 1)
    shares = [shares[0], partner(shares[1], "c")]
    shares = [share.reshape(8, 2, owned, width) for share in shares]
    live["attn_kept"], live["attn_sent"] = split(places, Y, shares, 1)
    live |= {"grad_heads": grad_heads, "weights_y": weights_y}
    live = fence(live)

    attn_y = partner(live.pop("attn_sent"), "y")
    kernel = functools.partial(attend_back_kernel, size, rings == 1)
    parts = projected + [live.pop("grad_heads"), logs, live["table"]]
    if rings == 1:
        grad_projected = call(
            kernel,
            "attend_back",
            [((span, 3 * wide), bf16)],
            places,
            *parts,
            scratch=[pltpu.VMEM((count, wide), f32)] * 2,
            mib=24,
            flops=40 * span * count * wide,
            exps=2 * span * count,
        )[0]
    else:
        outs = [((span, wide), bf16), ((count, wide), f32), ((count, wide), f32)]
        grad_q, grad_k, grad_v = call(kernel, "attend_back", outs, places, *parts, mib=36)
        grad_projected = call(
            functools.partial(turn_back_kernel, half),
            "turn_back",
            [((span, 3 * wide), bf16)],
            places,
            grad_q,
            ring_sums(grad_k),
            ring_sums(grad_v),
            live["table"],
        )[0]
    terms = call(
        project_back_kernel,
        "project_back",
        [((2 * block, width), bf16)] * 4,
        places,
        grad_projected,
        live["qkv"],
        flops=6 * span * width * wide,
    )
    live |= dict(zip(("kept_far", "sent_far", "kept_near", "sent_near"), terms))
    live["projected"] = grad_projected
    live |= {"result_x": result_x, "result_z": result_z, "result_both": result_both}
    live["attn_y"] = attn_y
    live = fence(live)

    over_x = partner(live.pop("sent_far"), "x")
    shares = [live.pop("weights_kept"), live.pop("weights_y")]
    shares = [share.reshape(1, 2, squares * owned, 3 * piece) for share in shares]
    live["weights_kept"], sent = split(places, ZH, shares, 1)
    weights_far = partner(sent, "zh")
    shape = (pairs, 2 * owned, 3 * wide)
    shares = call(
        project_outer_kernel,
        "project_outer",
        [(shape, bf16)] * 2 if direct else [((width, 3 * wide), bf16)],
        places,
        all_one,
        live.pop("projected"),
        flops=6 * span * width * wide,
    )
    if not direct:
        shares = split(places, C, [ring_sums(shares[0]).reshape(pairs, 2, 2 * owned, 3 * wide)], 1)
    shares = [shares[0], partner(shares[1], "c")]
    shares = [share.reshape(pairs, 2, owned, 3 * wide) for share in shares]
    live["qkv_kept"], live["qkv_sent"] = split(places, Y, shares, 1)
    shares = [share.reshape(2, 2, 2 * owned, width) for share in (live.pop("attn_kept"), live.pop("attn_y"))]
    live["attn_kept"], sent = split(places, ZL, shares, 1)
    live["attn_zl"] = partner(sent, "zl")
    live["sum6"], live["sum4"] = call(
        far_sums_kernel, "far_sums", [block_low] * 2, places, live.pop("kept_far"), over_x
    )
    live = fence(live)

    both = partner(live.pop("sum6"), "zl")
    over_x = partner(live.pop("sent_near"), "x")
    qkv_y = partner(live.pop("qkv_sent"), "y")
    shares = [share.reshape(2, 2, owned, width) for share in (live.pop("attn_kept"), live.pop("attn_zl"))]
    live["attn_kept"], sent = split(places, X, shares, 1)
    live["attn_x"] = partner(sent, "x")
    live["sum2"], live["sum0"], live["sum4"] = call(
        near_sums_kernel,
        "near_sums",
        [block_low] * 3,
        places,
        live.pop("kept_near"),
        over_x,
        live["sum4"],
        both,
    )
    live["qkv"] = total(places, live.pop("qkv_kept"), qkv_y)
    live = fence(live)

    far = partner(live.pop("sum4"), "zh")
    near = partner(live.pop("sum2"), "zl")
    shares = [share.reshape(squares, owned, 3 * piece) for share in (live.pop("weights_kept"), weights_far)]
    grad_packed = lax.all_to_all(total(places, *shares), square, 0, 0, tiled=True)
    shares = [share.reshape(1, 2, owned, width) for share in (live.pop("attn_kept"), live.pop("attn_x"))]
    kept_attn, sent = split(places, ZH, shares, 1)
    attn_zh = partner(sent, "zh")
    half_result, sent = call(
        result_kernel,
        "result",
        [half_low] * 2,
        places,
        live["middle"],
        live["result0"],
        live["result_x"],
        live["result_z"],
        live["result_both"],
    )
    output = call(
        leave_kernel, "leave", [(inputs.shape, bf16)], places, half_result, partner(sent, "c")
    )[0]
    live |= {"far": far, "near": near, "output": output, "grad_packed": grad_packed}
    live |= {"attn_kept": kept_attn, "attn_zh": attn_zh}
    live = fence(live)
    output, grad_packed = live["output"], live["grad_packed"]
    grad_qkv = lax.all_to_all(live.pop("qkv"), chips, 0, 0, tiled=True)
    grad_attn = (live["attn_kept"].astype(f32) + live["attn_zh"].astype(f32))[0]

    kept, sent = call(
        tokens_back_kernel,
        "tokens_back",
        [half_full] * 2,
        places,
        live["tokens"],
        live["grad_middle"],
        live["sum0"],
        live["near"],
        live["far"],
    )
    input_grad = call(
        leave_kernel, "leave", [(inputs.shape, f32)], places, kept, partner(sent, "c")
    )[0]

    grad_qkv = grad_qkv.astype(f32)
    grad_packed = grad_packed.astype(f32)
    grad_qkv = grad_qkv.reshape(pairs, owned, 3, wide)
    grad_qkv = grad_qkv.transpose(1, 2, 0, 3).reshape(owned, 3 * width)
    grad_gain_attn = jnp.sum(grad_qkv * w_qkv.astype(f32), axis=1)
    grad_qkv = grad_qkv * gain_one

    grad_in = jnp.concatenate(
        [
            columns_back(grad_packed[:, :, :piece], ff),
            columns_back(grad_packed[:, :, piece : 2 * piece], ff),
        ],
        axis=1,
    )
    grad_out = jnp.transpose(columns_back(grad_packed[:, :, 2 * piece :], ff))
    grad_gain_mlp = jnp.sum(grad_in * w_in.astype(f32), axis=1)
    grad_in = grad_in * gain_two
    return (
        output,
        input_grad,
        grad_gain_attn,
        grad_gain_mlp,
        grad_qkv,
        grad_attn,
        grad_in,
        grad_out,
    )


def solution(mesh):
    ctx, fsdp = mesh.shape["ctx"], mesh.shape["fsdp"]
    everyone = ("r", "zh", "zl", "x", "c", "y")
    grid = Mesh(mesh.devices.reshape(ctx // 16, 2, 2, 2, 2, fsdp), everyone)
    tokens = P("y", everyone[:-1], None)
    gain, rows, columns = P(everyone), P(everyone, None), P(None, everyone)
    return jax.shard_map(
        body,
        mesh=grid,
        in_specs=(tokens, gain, gain, rows, rows, rows, columns, tokens),
        out_specs=(tokens, tokens, gain, gain, rows, rows, rows, columns),
        check_vma=False,
    )
```

```python
import functools
import math

import jax
import jax.numpy as jnp
from jax import lax
from jax.experimental import pallas as pl
from jax.experimental.pallas import tpu as pltpu
from jax.sharding import Mesh
from jax.sharding import PartitionSpec as P

HEADS = 16
norm_eps = 1e-05
rope_base = 160000.0
f32 = jnp.float32
bf16 = jnp.bfloat16
LANES = 128
MIB = 1024 * 1024


def partner(array, axis):
    return lax.ppermute(array, axis, [(0, 1), (1, 0)])


def opposite(array, axes):
    return lax.ppermute(array, axes, [(i, 3 - i) for i in range(4)])


def after(array, *others):
    return lax.optimization_barrier((array, *others))[0]


class Taken:
    def __init__(self, arrays):
        self._arrays = arrays

    def __getattr__(self, name):
        return self._arrays.pop(name)


class Live:
    def __init__(self):
        self._held, self._due = {}, {}

    def __getattr__(self, name):
        return self._held[name]

    def put(self, due, **arrays):
        self._held.update(arrays)
        self._due.update(dict.fromkeys(arrays, due))

    @property
    def take(self):
        return Taken(self._held)

    def fence(self, stage):
        names = [name for name in self._held if self._due[name] <= stage]
        arrays = lax.optimization_barrier(tuple(self._held[name] for name in names))
        self._held.update(zip(names, arrays))


ROUND_1, ROUND_2, ROUND_3, ATTEND, RETURN, MIDDLE, SPREAD, FEED, CHIP, COLLECT, MIDDLE_BACK, LEAVE, ATTEND_BACK, OVER_X, OVER_ZL, OVER_ZH, LAST = range(17)
ENTER = -1
SCHEDULE = dict(
    qkv_pack=(ENTER, ENTER),
    qkv_slices=(ROUND_1, ROUND_2),
    qkv_y=(ROUND_3, ROUND_3),
    qkv_whole=(ROUND_3, ROUND_3),
    feed_pack=(ROUND_1, ROUND_1),
    feed_slices=(ROUND_2, ROUND_2),
    feed_zh=(ATTEND, RETURN),
    feed_y=(ATTEND, RETURN),
    feed_far_y=(MIDDLE, SPREAD),
    feed_whole=(SPREAD, SPREAD),
    attn_y=(ROUND_1, ROUND_2),
    attn_zh=(ROUND_2, ROUND_2),
    attn_zl=(ROUND_3, ROUND_3),
    attn_x=(ATTEND, ATTEND),
    attn_whole=(RETURN, RETURN),
    cot_over_x=(ROUND_1, ROUND_1),
    cot_over_z=(ROUND_3, ATTEND),
    cot_over_zx=(RETURN, RETURN),
    cot_cores=(FEED, FEED),
    tables=(ROUND_1, ROUND_2),
    rest=(COLLECT, COLLECT),
    result_sums=(LEAVE, ATTEND_BACK),
    result_x=(LEAVE, ATTEND_BACK),
    result_z=(LEAVE, ATTEND_BACK),
    result_both=(LEAVE, ATTEND_BACK),
    result_out=(OVER_ZH, OVER_ZH),
    grad_in_y=(COLLECT, LEAVE),
    grad_in_zh=(OVER_X, OVER_ZL),
    grad_in_slices=(OVER_ZH, OVER_ZH),
    grad_attn_made=(LEAVE, LEAVE),
    grad_attn_cut=(LEAVE, LEAVE),
    grad_attn_y=(ATTEND_BACK, OVER_ZH),
    grad_attn_zl=(OVER_X, OVER_X),
    grad_attn_x=(OVER_ZL, OVER_ZL),
    grad_attn_zh=(OVER_ZH, OVER_ZH),
    grad_qkv_made=(OVER_X, OVER_X),
    grad_qkv_y=(OVER_ZL, OVER_ZL),
    grad_qkv_slices=(LAST, LAST),
)
FENCES = set(range(ENTER, LAST))


def name_of(kernel):
    return kernel.func.__name__ if isinstance(kernel, functools.partial) else kernel.__name__


def add(*terms):
    total = terms[0].astype(f32)
    for term in terms[1:]:
        total = total + term.astype(f32)
    return total.astype(terms[0].dtype)


def call(kernel, outs, places, *arrays, scratch=(), mib=16, flops=0, exps=0):
    vmem = pl.BlockSpec(memory_space=pltpu.VMEM)
    moved = sum(array.size * array.dtype.itemsize for array in arrays)
    moved += sum(math.prod(shape) * jnp.dtype(dtype).itemsize for shape, dtype in outs)
    return pl.pallas_call(
        kernel,
        in_specs=[pl.BlockSpec(memory_space=pltpu.SMEM)] + [vmem] * len(arrays),
        out_specs=[vmem] * len(outs),
        out_shape=[jax.ShapeDtypeStruct(shape, dtype) for shape, dtype in outs],
        scratch_shapes=list(scratch),
        compiler_params=pltpu.CompilerParams(vmem_limit_bytes=mib * MIB),
        cost_estimate=pl.CostEstimate(flops=flops, bytes_accessed=moved, transcendentals=exps),
        name=name_of(kernel),
    )(places, *arrays)


CHIP, ZH, ZL, X, C, Y = range(6)


def nt(left, right):
    return lax.dot_general(left, right, (((1,), (1,)), ((), ())), preferred_element_type=f32)


def tn(left, right):
    return lax.dot_general(left, right, (((0,), (0,)), ((), ())), preferred_element_type=f32)


def nn(left, right):
    return lax.dot_general(left, right, (((1,), (0,)), ((), ())), preferred_element_type=f32)


def normalize(values):
    centre = values - jnp.mean(values, axis=-1, keepdims=True)
    inverse = lax.rsqrt(jnp.mean(centre * centre, axis=-1, keepdims=True) + norm_eps)
    return centre * inverse, inverse


def normalize_back(scaled, normed, inverse):
    inner = jnp.mean(scaled * normed, axis=-1, keepdims=True)
    return inverse * (scaled - jnp.mean(scaled, axis=-1, keepdims=True) - normed * inner)


def pick_kernel(places, own_ref, other_ref, block_ref):
    half = own_ref.shape[1]
    block_ref[:half, :] = own_ref[places[C]]
    block_ref[half:, :] = other_ref[places[C]]


def enter_kernel(places, own_ref, other_ref, cot_a_ref, cot_b_ref, block_ref, cot_ref, low_ref):
    pick_kernel(places, own_ref, other_ref, block_ref)
    pick_kernel(places, cot_a_ref, cot_b_ref, cot_ref)
    low_ref[...] = normalize(block_ref[...].astype(f32))[0].astype(bf16)


def leave_kernel(places, own_ref, other_ref, out_ref):
    out_ref[places[C]] = own_ref[...]
    out_ref[1 - places[C]] = other_ref[...]


def assemble_kernel(lead, first, second, places, a_ref, b_ref, c_ref, d_ref, out_ref):
    chip = places[lead] if lead is not None else 0
    one, two = places[first], places[second]
    for i, row in enumerate(((a_ref, b_ref), (c_ref, d_ref))):
        for j, ref in enumerate(row):
            for at in range(ref.shape[0]):
                out_ref[chip ^ at, one ^ i, :, two ^ j] = ref[at]


def assemble(places, lead, first, second, pieces):
    extent = pieces[0].shape
    shape = (extent[0], 2, extent[1], 2) + extent[2:]
    if extent[2] % 16 == 0:
        kernel = functools.partial(assemble_kernel, lead, first, second)
        return call(kernel, [(shape, bf16)], places, *pieces)[0]

    def ordered(own, other, place, axis):
        straight = jnp.stack([own, other], axis)
        return jnp.where(place == 0, straight, jnp.flip(straight, axis))

    one = ordered(pieces[0], pieces[1], places[second], 2)
    two = ordered(pieces[2], pieces[3], places[second], 2)
    whole = ordered(one, two, places[first], 1)
    if lead is None:
        return whole
    return jnp.take(whole, jnp.arange(extent[0]) ^ places[lead], axis=0)


def assemble_rows_kernel(places, a_ref, b_ref, c_ref, d_ref, out_ref):
    for i, row in enumerate(((a_ref, b_ref), (c_ref, d_ref))):
        for j, ref in enumerate(row):
            for at in range(4):
                for k in range(2):
                    out_ref[places[CHIP] ^ (2 * at + j), places[C] ^ i, places[Y] ^ k] = ref[at, k]


def assemble_rows(places, pieces):
    if pieces[0].shape[2] % 16 == 0:
        shape = (8, 2) + pieces[0].shape[1:]
        return call(assemble_rows_kernel, [(shape, bf16)], places, *pieces)[0]
    merged = [jnp.stack(pieces[at : at + 2], axis=1) for at in (0, 2)]
    merged = [member.reshape((8, 1) + member.shape[2:]) for member in merged]
    pieces = [member[:, :, at] for member in merged for at in range(2)]
    return assemble(places, CHIP, C, Y, pieces)


def total_kernel(places, a_ref, b_ref, out_ref):
    out_ref[...] = (a_ref[...].astype(f32) + b_ref[...].astype(f32)).astype(bf16)


def total(places, kept, other):
    if kept.shape[1] % 16 == 0:
        return call(total_kernel, [(kept.shape, bf16)], places, kept, other)[0]
    return add(kept, other)


def put_shares(made, place, at, kept_ref, sent_ref):
    share, width = kept_ref.shape[1:]
    groups = made.shape[0] // (2 * share)
    made = made.reshape(groups, 2, share, width)
    kept_ref[pl.ds(at, groups)] = jnp.where(place == 0, made[:, 0], made[:, 1]).astype(bf16)
    sent_ref[pl.ds(at, groups)] = jnp.where(place == 0, made[:, 1], made[:, 0]).astype(bf16)


def split_kernel(which, count, places, *refs):
    kept_ref, sent_ref = refs[count:]
    place = places[which]
    for ref, at in ((kept_ref, place), (sent_ref, 1 - place)):
        total = refs[0][:, at]
        if count > 1:
            total = total.astype(f32)
            for term in refs[1:count]:
                total = total + term[:, at].astype(f32)
        ref[...] = total.astype(bf16)


def split(places, which, parts, before):
    shape = parts[0].shape
    rest = shape[:before] + shape[before + 1 :]
    if shape[-2] % 16 == 0:
        flat = (math.prod(shape[:before]), 2, math.prod(shape[before + 1 : -1]), shape[-1])
        outs = [((flat[0],) + flat[2:], bf16)] * 2
        kernel = functools.partial(split_kernel, which, len(parts))
        halves = call(kernel, outs, places, *[part.reshape(flat) for part in parts])
        return [half.reshape(rest) for half in halves]
    total = add(*parts)
    return [
        lax.dynamic_index_in_dim(total, at, before, False)
        for at in (places[which], 1 - places[which])
    ]


def halves_swapped(values, half):
    lane = lax.broadcasted_iota(jnp.int32, values.shape, 1)
    up = pltpu.roll(values, half, 1)
    down = pltpu.roll(values, values.shape[1] - half, 1)
    return jnp.where(lane % (2 * half) < half, down, up)


def project_kernel(half, places, *refs):
    pieces, (weight_ref, table_ref, out_ref, stack_ref) = refs[:8], refs[8:]
    width = out_ref.shape[1] // 3
    rows = pieces[0].shape[0]
    for at in range(0, 8, 2):
        here = pl.ds(at * rows, 2 * rows)
        both = jnp.concatenate([ref[...] for ref in pieces[at : at + 2]])
        stack_ref[here, :] = both
        made = nn(both, weight_ref[...])
        cosine, sine = table_ref[here, :width], table_ref[here, width:]
        for place in range(2):
            part = made[:, place * width : (place + 1) * width]
            turned = part * cosine + halves_swapped(part, half) * sine
            out_ref[here, place * width : (place + 1) * width] = turned.astype(bf16)
        out_ref[here, 2 * width :] = made[:, 2 * width :].astype(bf16)


def of_head(values, head, size):
    lane = lax.broadcasted_iota(jnp.int32, values.shape, 1)
    return jnp.where(lane // size == head, values, jnp.zeros_like(values))


def keys_and_values(refs, width):
    if len(refs) == 1:
        return refs[0][:, width : 2 * width], refs[0][:, 2 * width :]
    return refs[1][:, :width], refs[1][:, width:]


def attend_kernel(size, places, *refs):
    refs, (o_ref, log_ref) = refs[:-2], refs[-2:]
    block, width = o_ref.shape[1:]
    keys, values = keys_and_values(refs, width)
    step = log_ref.shape[2]
    scale = math.log2(math.e) / math.sqrt(size)

    def visit(i, carry):
        queries = refs[0][pl.ds(pl.multiple_of(i * step, step), step), :width]
        outs = []
        for head in range(width // size):
            scores = nt(keys, of_head(queries, head, size))
            top = jnp.max(scores, axis=0, keepdims=True)
            weights = jnp.exp2((scores - top) * scale)
            total = jnp.sum(weights, axis=0, keepdims=True)
            probs = (weights * (1.0 / total)).astype(bf16)
            outs.append(tn(values, probs)[head * size : (head + 1) * size])
            log_ref[i, head : head + 1, :] = top * scale + jnp.log2(total)
        out = jnp.transpose(jnp.concatenate(outs, axis=0)).astype(bf16)
        for at in range(step // block):
            chip = places[CHIP] ^ (i * (step // block) + at)
            o_ref[chip] = out[at * block : (at + 1) * block]
        return carry

    lax.fori_loop(0, refs[0].shape[0] // step, visit, 0)


def attend_back_kernel(size, together, places, *refs):
    refs, (grad_ref, log_ref, table_ref, dq_ref, dk_ref, dv_ref) = refs[:-6], refs[-6:]
    block, width = grad_ref.shape[1:]
    keys, values = keys_and_values(refs, width)
    step = log_ref.shape[2]
    scale = 1.0 / math.sqrt(size)
    exponent = scale * math.log2(math.e)
    dk_ref[...] = jnp.zeros_like(dk_ref)
    dv_ref[...] = jnp.zeros_like(dv_ref)

    def turned(part, here):
        back = halves_swapped(part, size // 2) * table_ref[here, width:]
        return (part * table_ref[here, :width] - back).astype(bf16)

    def visit(i, carry):
        here = pl.ds(pl.multiple_of(i * step, step), step)
        queries = refs[0][here, :width]
        grads = [grad_ref[places[CHIP] ^ (i * (step // block) + at)] for at in range(step // block)]
        grads = jnp.concatenate(grads)
        outs = []
        for head in range(width // size):
            query, grad = of_head(queries, head, size), of_head(grads, head, size)
            probs = jnp.exp2(nt(keys, query) * exponent - log_ref[i, head : head + 1, :])
            grad_probs = nt(values, grad)
            delta = jnp.sum(probs * grad_probs, axis=0, keepdims=True)
            grad_scores = (probs * (grad_probs - delta)).astype(bf16)
            outs.append(tn(keys, grad_scores)[head * size : (head + 1) * size])
            dk_ref[...] += nn(grad_scores, query)
            dv_ref[...] += nn(probs.astype(bf16), grad)
        dq = jnp.transpose(jnp.concatenate(outs, axis=0)) * scale
        dq_ref[here, :width] = turned(dq, here)
        return carry

    lax.fori_loop(0, refs[0].shape[0] // step, visit, 0)
    if together:
        everything = pl.ds(0, dq_ref.shape[0])
        dq_ref[:, width : 2 * width] = turned(dk_ref[...] * scale, everything)
        dq_ref[:, 2 * width :] = dv_ref[...].astype(bf16)
    else:
        dk_ref[...] = dk_ref[...] * scale


def turn_back_kernel(half, places, dq_ref, dk_ref, dv_ref, table_ref, out_ref):
    width = dq_ref.shape[1]
    part = dk_ref[...]
    back = halves_swapped(part, half) * table_ref[:, width:]
    out_ref[:, :width] = dq_ref[...]
    out_ref[:, width : 2 * width] = (part * table_ref[:, :width] - back).astype(bf16)
    out_ref[:, 2 * width :] = dv_ref[...].astype(bf16)


def middle_kernel(places, arrived_ref, weight_ref, tokens_ref, attended_ref, middle_ref, low_ref):
    wide = arrived_ref.shape[2]
    for at in range(arrived_ref.shape[0]):
        attended_ref[:, at * wide : (at + 1) * wide] = arrived_ref[at]
    middle = tokens_ref[...].astype(f32) + nn(attended_ref[...], weight_ref[...])
    middle_ref[...] = middle
    low_ref[...] = normalize(middle)[0].astype(bf16)


def feed_kernel(places, *refs):
    two, cot, (w_ref, hidden_ref, grad_ref), outs = refs[:8], refs[8:16], refs[16:19], refs[19:]
    piece = hidden_ref.shape[1]
    rows = two[0].shape[0]
    w_in, w_out = w_ref[:, : 2 * piece], w_ref[:, 2 * piece :]
    for at in (4, 6, 0, 2):
        here = pl.ds(at * rows, 2 * rows)
        gate_up = nn(jnp.concatenate([two[at][...], two[at + 1][...]]), w_in)
        grad_hidden = nn(jnp.concatenate([cot[at][...], cot[at + 1][...]]), w_out)
        gate, lift = gate_up[:, :piece], gate_up[:, piece:]
        cdf = 0.5 * (1.0 + lax.erf(gate * math.sqrt(0.5)))
        density = jnp.exp(-0.5 * gate * gate) * (1.0 / math.sqrt(2.0 * math.pi))
        activated = gate * cdf
        hidden_ref[here, :] = (activated * lift).astype(bf16)
        grad_gate = (grad_hidden * lift * (cdf + gate * density)).astype(bf16)
        grad_lift = (grad_hidden * activated).astype(bf16)
        grad_ref[here, :piece] = grad_gate
        grad_ref[here, piece:] = grad_lift
        made = nt(grad_gate, w_in[:, :piece]) + nt(grad_lift, w_in[:, piece:])
        outs[at // 4][pl.ds(at % 4 * rows, 2 * rows), :] = made.astype(bf16)


def feed(places, two, cot, weights):
    rows, width = two[0].shape
    piece = weights.shape[1] // 3
    outs = [((8 * rows, piece), bf16), ((8 * rows, 2 * piece), bf16)] + [((4 * rows, width), bf16)] * 2
    hidden, grads, *terms = call(
        feed_kernel,
        outs,
        places,
        *two,
        *cot,
        weights,
        mib=24,
        flops=80 * rows * width * piece,
        exps=16 * rows * piece,
    )
    return hidden, grads, terms


def feed_rest_kernel(places, *refs):
    two, cot, (hidden_ref, grad_ref, w_ref), outs, made_refs = (
        refs[:8],
        refs[8:16],
        refs[16:19],
        refs[19:21],
        refs[21:],
    )
    piece = hidden_ref.shape[1]
    rows, width = two[0].shape
    w_out = w_ref[:, 2 * piece :]
    for at in (4, 6, 0, 2):
        made = nt(hidden_ref[pl.ds(at * rows, 2 * rows), :], w_out)
        outs[at // 4][pl.ds(at % 4 * rows, 2 * rows), :] = made.astype(bf16)
    step = width // 4
    for at in range(0, width, step):
        here = pl.ds(at, step)
        left = jnp.concatenate([ref[:, here] for ref in two])
        made = tn(left, grad_ref[...])
        left = jnp.concatenate([ref[:, here] for ref in cot])
        made = jnp.concatenate([made, tn(left, hidden_ref[...])], axis=1)
        if len(made_refs) == 1:
            made_refs[0][here, :] = made.astype(bf16)
        else:
            put_shares(made, places[Y], at // (2 * made_refs[0].shape[1]), *made_refs)


def feed_rest(places, two, cot, hidden, grads, weights, shares):
    rows, width = two[0].shape
    outs = [((4 * rows, width), bf16)] * 2 + [(shape, bf16) for shape in shares]
    made = call(
        feed_rest_kernel,
        outs,
        places,
        *two,
        *cot,
        hidden,
        grads,
        weights,
        mib=24,
        flops=64 * rows * width * (weights.shape[1] // 3),
    )
    return made[:2], made[2:]


def chip_sums_kernel(places, a_ref, b_ref, *outs):
    rows = outs[0].shape[0]
    for at, ref in enumerate(outs):
        here = pl.ds(at * rows, rows)
        ref[...] = (a_ref[here, :].astype(f32) + b_ref[here, :].astype(f32)).astype(bf16)


def chip_sums(places, here, there):
    shape = (here.shape[0] // 4, here.shape[1])
    return call(chip_sums_kernel, [(shape, bf16)] * 4, places, here, partner(there, "c"))


def far_sums_kernel(places, kept_ref, across_ref, six_ref, four_ref):
    rows = six_ref.shape[0]
    for at, ref in enumerate((six_ref, four_ref)):
        here = pl.ds(at * rows, rows)
        ref[...] = (kept_ref[here, :].astype(f32) + across_ref[here, :].astype(f32)).astype(bf16)


def near_sums_kernel(places, kept_ref, across_ref, four_ref, both_ref, two_ref, own_ref, out_ref):
    far_sums_kernel(places, kept_ref, across_ref, two_ref, own_ref)
    out_ref[...] = (four_ref[...].astype(f32) + both_ref[...].astype(f32)).astype(bf16)


def result_kernel(places, middle_ref, a_ref, b_ref, c_ref, d_ref, kept_ref, sent_ref):
    total = middle_ref[...]
    for ref in (a_ref, b_ref, c_ref, d_ref):
        total = total + ref[...].astype(f32)
    total = total.astype(bf16)
    half = kept_ref.shape[0]
    kept_ref[...] = total[:half]
    sent_ref[...] = total[half:]


def middle_back_kernel(
    places, middle_ref, cot_ref, weight_ref, a_ref, b_ref, c_ref, d_ref, grad_ref, low_ref, leaving_ref
):
    scaled = a_ref[...].astype(f32)
    for ref in (b_ref, c_ref, d_ref):
        scaled = scaled + ref[...].astype(f32)
    normed, inverse = normalize(middle_ref[...])
    grad = cot_ref[...].astype(f32) + normalize_back(scaled, normed, inverse)
    grad_ref[...] = grad
    low = grad.astype(bf16)
    low_ref[...] = low
    made = nt(low, weight_ref[...]).astype(bf16)
    wide = leaving_ref.shape[2]
    for at in range(leaving_ref.shape[0]):
        leaving_ref[at] = made[:, at * wide : (at + 1) * wide]


def outer_kernel(places, left_ref, right_ref, *made_refs):
    made = tn(left_ref[...], right_ref[...])
    if len(made_refs) == 1:
        made_refs[0][...] = made.astype(bf16)
    else:
        put_shares(made, places[C], 0, *made_refs)


def project_back_kernel(places, grad_ref, weight_ref, *outs):
    rows = outs[0].shape[0] // 2
    for at in (6, 4, 2, 0):
        made = nt(grad_ref[pl.ds(at * rows, 2 * rows), :], weight_ref[...]).astype(bf16)
        first = 0 if at >= 4 else 2
        here = pl.ds((0 if at in (6, 2) else 1) * rows, rows)
        outs[first][here, :] = made[:rows]
        outs[first + 1][here, :] = made[rows:]


def project_outer_kernel(places, left_ref, grad_ref, *made_refs):
    width = left_ref.shape[1]
    step = width // 4
    for at in range(0, width, step):
        made = tn(left_ref[:, pl.ds(at, step)], grad_ref[...])
        if len(made_refs) == 1:
            made_refs[0][pl.ds(at, step), :] = made.astype(bf16)
        else:
            put_shares(made, places[C], at // (2 * made_refs[0].shape[1]), *made_refs)


def tokens_back_kernel(places, tokens_ref, grad_ref, a_ref, b_ref, c_ref, kept_ref, sent_ref):
    scaled = a_ref[...].astype(f32)
    for ref in (b_ref, c_ref):
        scaled = scaled + ref[...].astype(f32)
    normed, inverse = normalize(tokens_ref[...].astype(f32))
    total = grad_ref[...] + normalize_back(scaled, normed, inverse)
    half = kept_ref.shape[0]
    kept_ref[...] = total[:half]
    sent_ref[...] = total[half:]


def columns_by(array, pieces, piece):
    rows, count = array.shape
    padded = jnp.pad(array, ((0, 0), (0, pieces * piece - count)))
    return jnp.swapaxes(padded.reshape(rows, pieces, piece), 0, 1)


def columns_back(array, count):
    pieces, rows, piece = array.shape
    return jnp.swapaxes(array, 0, 1).reshape(rows, pieces * piece)[:, :count]


def body(inputs, gain_attn, gain_mlp, w_qkv, w_attn_out, w_in, w_out, cotangent):
    pairs, squares = 8, 8
    rings = lax.axis_size("r")
    seqs, half_block, width = inputs.shape
    owned = w_qkv.shape[0]
    size = width // HEADS
    half = size // 2
    wide = width // pairs
    block = seqs * half_block
    span = pairs * block
    ff = w_out.shape[0]
    piece = -(-ff // (squares * LANES)) * LANES
    chips, square = ("zh", "zl", "x"), ("zl", "x", "c")
    everyone = ("r",) + chips + ("c", "y")
    ri, zh, zl, xi, ci, yi = (lax.axis_index(name) for name in everyone)
    places = jnp.stack([4 * zh + 2 * zl + xi, zh, zl, xi, ci, yi]).astype(jnp.int32)
    block_low, half_low = ((block, width), bf16), ((half_block, width), bf16)
    block_full, half_full = ((block, width), f32), ((half_block, width), f32)

    def over_rings(array):
        return lax.all_gather(array, "r", axis=0) if rings > 1 else array

    def ring_sums(array):
        if rings > 1:
            return lax.psum_scatter(array, "r", scatter_dimension=0, tiled=True)
        return array

    gain_one = gain_attn.astype(f32)[:, None]
    gain_two = gain_mlp.astype(f32)[:, None]
    count = rings * span
    direct = rings == 1 and owned % 16 == 0

    live = Live()
    steps = []

    def step(made):
        steps.append((SCHEDULE[made.__name__], made))

    def begin(stage):
        for at, ((start, due), made) in enumerate(steps):
            if start == stage:
                steps[at] = ((None, due), made)
                live.put(due, **made())

    def reach(stage):
        begin(stage)
        if stage in FENCES:
            live.fence(stage)


    @step
    def qkv_pack():
        scaled = (live.take.w_qkv.astype(f32) * gain_one).astype(bf16)
        slices = scaled.reshape(owned, 3, pairs, wide).transpose(2, 0, 1, 3)
        return dict(slices=slices.reshape(pairs, owned, 3 * wide))

    @step
    def qkv_slices():
        return dict(qkv_own=lax.all_to_all(live.take.slices, chips, 0, 0, tiled=True)[:, None])

    @step
    def qkv_y():
        return dict(qkv_other=partner(live.qkv_own, "y"))

    @step
    def qkv_whole():
        parts = [live.take.qkv_own, live.take.qkv_other]
        parts = parts + [partner(part, "c") for part in parts]
        return dict(qkv=over_rings(assemble(places, None, C, Y, parts)).reshape(width, 3 * wide))


    @step
    def feed_pack():
        scaled = (live.take.w_in.astype(f32) * gain_two).astype(bf16)
        packed = [
            columns_by(scaled[:, :ff], squares, piece),
            columns_by(scaled[:, ff:], squares, piece),
            columns_by(jnp.transpose(live.take.w_out), squares, piece),
        ]
        return dict(packed=jnp.concatenate(packed, axis=2))

    @step
    def feed_slices():
        return dict(packed=lax.all_to_all(live.take.packed, square, 0, 0, tiled=True)[None])

    @step
    def feed_zh():
        return dict(packed_far=partner(live.packed, "zh"))

    @step
    def feed_y():
        return dict(packed_y=partner(live.packed, "y"))

    @step
    def feed_far_y():
        return dict(packed_far_y=partner(live.packed_far, "y"))

    @step
    def feed_whole():
        take = live.take
        parts = [take.packed, take.packed_y, take.packed_far, take.packed_far_y]
        whole = assemble(places, None, ZH, Y, parts)
        return dict(weights=over_rings(whole).reshape(width, 3 * piece))


    @step
    def attn_y():
        return dict(full=jnp.stack([live.w_attn_out, partner(live.take.w_attn_out, "y")]))

    @step
    def attn_zh():
        return dict(full=jnp.stack([live.full, partner(live.full, "zh")]))

    @step
    def attn_zl():
        return dict(full=jnp.stack([live.full, partner(live.full, "zl")], axis=1))

    @step
    def attn_x():
        return dict(full_x=partner(live.full, "x"))

    @step
    def attn_whole():
        parts = [part.reshape(4, 2, owned, width) for part in (live.take.full, live.take.full_x)]
        parts = parts + [partner(part, "c") for part in parts]
        return dict(attn=over_rings(assemble_rows(places, parts)).reshape(width, width))


    @step
    def cot_over_x():
        return dict(cot_x=partner(live.cot, "x"))

    @step
    def cot_over_z():
        return dict(cot_z=partner(live.cot, "zl"))

    @step
    def cot_over_zx():
        return dict(cot_zx=partner(live.cot_z, "x"))

    @step
    def cot_cores():
        parts = (live.cot, live.cot_x, live.cot_z, live.cot_zx)
        own, over_x, over_z, over_zx = (partner(part, "c") for part in parts)
        return dict(core=own, core_x=over_x, core_z=over_z, core_zx=over_zx)

    @step
    def tables():
        lane = jnp.arange(wide, dtype=jnp.int32)
        frequency = rope_base ** (-2.0 * (lane % half).astype(f32) / size)
        sign = jnp.where(lane % size < half, -1.0, 1.0)
        row = jnp.arange(span, dtype=jnp.int32)
        chip = (live.places[CHIP] ^ (row // block)) * block
        core = (live.places[C] ^ (row % block // half_block)) * half_block
        at = ri * span + chip + core + row % half_block
        angles = at.astype(f32)[:, None] * frequency[None, :]
        return dict(table=jnp.concatenate([jnp.cos(angles), jnp.sin(angles) * sign], axis=1))


    @step
    def rest():
        shape = (2 * squares, owned, 3 * piece)
        result, shares = feed_rest(
            places,
            all_two,
            all_cotangent(),
            live.take.hidden,
            live.take.gate_up,
            live.take.weights,
            [shape] * 2 if direct else [(width, 3 * piece)],
        )
        if not direct:
            terms = ring_sums(shares[0]).reshape(2 * squares, 2, owned, 3 * piece)
            shares = split(places, Y, [terms], 1)
        return dict(
            result_here=result[0],
            result_there=result[1],
            weights_kept=shares[0],
            weights_sent=shares[1],
        )

    @step
    def result_sums():
        sums = chip_sums(places, live.take.result_here, live.take.result_there)
        return dict(result0=sums[0], result1=sums[1], result2=sums[2], result3=sums[3])

    @step
    def result_x():
        return dict(result1=partner(live.result1, "x"))

    @step
    def result_z():
        return dict(result2=partner(live.result2, "zl"))

    @step
    def result_both():
        return dict(result3=opposite(live.result3, ("zl", "x")))

    @step
    def result_out():
        take = live.take
        kept, sent = call(
            result_kernel,
            [half_low] * 2,
            places,
            live.middle,
            take.result0,
            take.result1,
            take.result2,
            take.result3,
        )
        out = call(leave_kernel, [(inputs.shape, bf16)], places, kept, partner(sent, "c"))[0]
        return dict(output=out)

    @step
    def grad_in_y():
        return dict(weights_y=partner(live.take.weights_sent, "y"))

    @step
    def grad_in_zh():
        shares = [live.take.weights_kept, live.take.weights_y]
        shares = [share.reshape(1, 2, squares * owned, 3 * piece) for share in shares]
        kept, sent = split(places, ZH, shares, 1)
        return dict(weights_kept=kept, weights_far=partner(sent, "zh"))

    @step
    def grad_in_slices():
        shares = [live.take.weights_kept, live.take.weights_far]
        shares = [share.reshape(squares, owned, 3 * piece) for share in shares]
        return dict(grad_packed=lax.all_to_all(total(places, *shares), square, 0, 0, tiled=True))


    @step
    def grad_attn_made():
        shape = (pairs, 2 * owned, width)
        shares = call(
            outer_kernel,
            [(shape, bf16)] * 2 if direct else [((width, width), bf16)],
            places,
            live.take.attended,
            live.take.branch,
        )
        if not direct:
            terms = ring_sums(shares[0]).reshape(pairs, 2, 2 * owned, width)
            shares = split(places, C, [terms], 1)
        return dict(attn_kept=shares[0], attn_other=partner(shares[1], "c"))

    def attn_sums(which, before, after_it, name):
        shares = [live.take.attn_kept, live.take.attn_other]
        shares = [share.reshape(before, 2, after_it * owned, width) for share in shares]
        kept, sent = split(places, which, shares, 1)
        return dict(attn_kept=kept, attn_other=partner(sent, name))

    @step
    def grad_attn_cut():
        shares = [live.take.attn_kept, live.take.attn_other]
        shares = [share.reshape(8, 2, owned, width) for share in shares]
        kept, sent = split(places, Y, shares, 1)
        return dict(attn_kept=kept, attn_sent=sent)

    @step
    def grad_attn_y():
        return dict(attn_other=partner(live.take.attn_sent, "y"))

    @step
    def grad_attn_zl():
        return attn_sums(ZL, 2, 2, "zl")

    @step
    def grad_attn_x():
        return attn_sums(X, 2, 1, "x")

    @step
    def grad_attn_zh():
        return attn_sums(ZH, 1, 1, "zh")


    @step
    def grad_qkv_made():
        shape = (pairs, 2 * owned, 3 * wide)
        shares = call(
            project_outer_kernel,
            [(shape, bf16)] * 2 if direct else [((width, 3 * wide), bf16)],
            places,
            all_one,
            live.take.projected,
        )
        if not direct:
            terms = ring_sums(shares[0]).reshape(pairs, 2, 2 * owned, 3 * wide)
            shares = split(places, C, [terms], 1)
        shares = [shares[0], partner(shares[1], "c")]
        shares = [share.reshape(pairs, 2, owned, 3 * wide) for share in shares]
        kept, sent = split(places, Y, shares, 1)
        return dict(qkv_kept=kept, qkv_sent=sent)

    @step
    def grad_qkv_y():
        return dict(qkv_kept=total(places, live.take.qkv_kept, partner(live.take.qkv_sent, "y")))

    @step
    def grad_qkv_slices():
        return dict(grad_qkv=lax.all_to_all(live.take.qkv_kept, chips, 0, 0, tiled=True))

    tokens, cot, low_one = call(
        enter_kernel,
        [block_low] * 3,
        places,
        inputs,
        partner(inputs, "c"),
        cotangent,
        partner(cotangent, "c"),
    )
    live.put(-1, tokens=tokens, cot=cot, one0=low_one, places=places)
    live.put(-1, w_qkv=w_qkv, w_attn_out=w_attn_out, w_in=w_in, w_out=w_out)
    reach(-1)

    one1, one2, one4 = (partner(live.one0, name) for name in ("x", "zl", "zh"))
    live.put(ROUND_1, one1=one1, one2=one2, one4=one4)
    reach(ROUND_1)
    places = live.places

    one3, one5, one6 = partner(live.one2, "x"), partner(live.one4, "x"), partner(live.one4, "zl")
    live.put(ROUND_2, one3=one3, one5=one5, one6=one6)
    reach(ROUND_2)

    live.put(ROUND_3, one7=partner(live.one6, "x"))
    reach(ROUND_3)

    take = live.take
    parts = [take.one0, take.one1, take.one2, take.one3, take.one4, take.one5, take.one6, take.one7]
    projected, all_one = call(
        functools.partial(project_kernel, half),
        [((span, 3 * wide), bf16), ((span, width), bf16)],
        places,
        *parts,
        live.qkv,
        live.table,
    )
    projected = [projected]
    if rings > 1:
        projected += [lax.all_gather(projected[0][:, wide:], "r", axis=0, tiled=True)]
    rows = 2 * block if count <= 2048 else block
    heads_out, logs = call(
        functools.partial(attend_kernel, size),
        [((pairs, block, wide), bf16), ((span // rows, 8, rows), f32)],
        places,
        *projected,
        mib=24,
    )
    live.put(ATTEND, heads=heads_out)
    reach(ATTEND)

    live.put(RETURN, arrived=lax.all_to_all(live.take.heads, chips, 0, 0, tiled=True))
    reach(RETURN)

    attended, middle, low_two = call(
        middle_kernel,
        [block_low, block_full, block_low],
        places,
        live.take.arrived,
        live.attn,
        live.tokens,
    )
    live.put(MIDDLE, attended=attended, middle=middle, two=low_two)
    reach(MIDDLE)

    over_x, over_z = partner(live.two, "x"), partner(live.two, "zl")
    live.put(SPREAD, over_x=over_x, over_z=over_z, over_both=opposite(live.two, ("zl", "x")))
    reach(SPREAD)

    def all_cotangent():
        here = [live.cot, live.cot_x, live.cot_z, live.cot_zx]
        return here + [live.core, live.core_x, live.core_z, live.core_zx]

    all_two = [live.take.two, live.take.over_x, live.take.over_z, live.take.over_both]
    all_two += [partner(member, "c") for member in all_two]
    begin(FEED)
    hidden, grad_gate_up, terms = feed(places, all_two, all_cotangent(), live.weights)
    live.put(FEED, hidden=hidden, gate_up=grad_gate_up, here=terms[0], there=terms[1])
    reach(FEED)

    sums = chip_sums(places, live.take.here, live.take.there)
    live.put(CHIP, sum0=sums[0], sum1=sums[1], sum2=sums[2], sum3=sums[3])
    reach(CHIP)

    over_both = opposite(live.take.sum3, ("zl", "x"))
    over_x, over_z = partner(live.take.sum1, "x"), partner(live.take.sum2, "zl")
    live.put(COLLECT, sum1=over_x, sum2=over_z, sum3=over_both)
    reach(COLLECT)

    take = live.take
    grad_middle, grad_branch, leaving = call(
        middle_back_kernel,
        [block_full, block_low, ((pairs, block, wide), bf16)],
        places,
        live.middle,
        live.cot,
        live.attn,
        take.sum0,
        take.sum1,
        take.sum2,
        take.sum3,
    )
    live.put(MIDDLE_BACK, grad_middle=grad_middle, branch=grad_branch, leaving=leaving)
    reach(MIDDLE_BACK)

    live.put(LEAVE, grad_heads=lax.all_to_all(live.take.leaving, chips, 0, 0, tiled=True))
    reach(LEAVE)

    kernel = functools.partial(attend_back_kernel, size, rings == 1)
    parts = projected + [live.take.grad_heads, logs, live.table]
    if rings == 1:
        grad_projected = call(
            kernel,
            [((span, 3 * wide), bf16)],
            places,
            *parts,
            scratch=[pltpu.VMEM((count, wide), f32)] * 2,
            mib=24,
        )[0]
    else:
        outs = [((span, wide), bf16), ((count, wide), f32), ((count, wide), f32)]
        grad_q, grad_k, grad_v = call(kernel, outs, places, *parts, mib=36)
        grad_projected = call(
            functools.partial(turn_back_kernel, half),
            [((span, 3 * wide), bf16)],
            places,
            grad_q,
            ring_sums(grad_k),
            ring_sums(grad_v),
            live.table,
        )[0]
    terms = call(
        project_back_kernel, [((2 * block, width), bf16)] * 4, places, grad_projected, live.qkv
    )
    live.put(ATTEND_BACK, projected=grad_projected, kept_far=terms[0], sent_far=terms[1])
    live.put(ATTEND_BACK, kept_near=terms[2], sent_near=terms[3])
    reach(ATTEND_BACK)

    over_x = partner(live.take.sent_far, "x")
    six, four = call(far_sums_kernel, [block_low] * 2, places, live.take.kept_far, over_x)
    live.put(OVER_X, six=six, four=four)
    reach(OVER_X)

    both = partner(live.take.six, "zl")
    over_x = partner(live.take.sent_near, "x")
    two, own, four = call(
        near_sums_kernel,
        [block_low] * 3,
        places,
        live.take.kept_near,
        over_x,
        live.take.four,
        both,
    )
    live.put(OVER_ZL, two=two, own=own, four=four)
    reach(OVER_ZL)

    live.put(OVER_ZH, far=partner(live.take.four, "zh"), near=partner(live.take.two, "zl"))
    reach(OVER_ZH)

    kept, sent = call(
        tokens_back_kernel,
        [half_full] * 2,
        places,
        live.tokens,
        live.grad_middle,
        live.own,
        live.near,
        live.far,
    )
    input_grad = call(leave_kernel, [(inputs.shape, f32)], places, kept, partner(sent, "c"))[0]
    reach(LAST)

    grad_attn = (live.attn_kept.astype(f32) + live.attn_other.astype(f32))[0]
    grad_qkv = live.grad_qkv.astype(f32).reshape(pairs, owned, 3, wide)
    grad_qkv = grad_qkv.transpose(1, 2, 0, 3).reshape(owned, 3 * width)
    grad_gain_attn = jnp.sum(grad_qkv * w_qkv.astype(f32), axis=1)
    grad_qkv = grad_qkv * gain_one

    grad_packed = live.grad_packed.astype(f32)
    grad_in = jnp.concatenate(
        [
            columns_back(grad_packed[:, :, :piece], ff),
            columns_back(grad_packed[:, :, piece : 2 * piece], ff),
        ],
        axis=1,
    )
    grad_out = jnp.transpose(columns_back(grad_packed[:, :, 2 * piece :], ff))
    grad_gain_mlp = jnp.sum(grad_in * w_in.astype(f32), axis=1)
    grad_in = grad_in * gain_two
    return (
        live.output,
        input_grad,
        grad_gain_attn,
        grad_gain_mlp,
        grad_qkv,
        grad_attn,
        grad_in,
        grad_out,
    )


def solution(mesh):
    ctx, fsdp = mesh.shape["ctx"], mesh.shape["fsdp"]
    everyone = ("r", "zh", "zl", "x", "c", "y")
    grid = Mesh(mesh.devices.reshape(ctx // 16, 2, 2, 2, 2, fsdp), everyone)
    tokens = P("y", everyone[:-1], None)
    gain, rows, columns = P(everyone), P(everyone, None), P(None, everyone)
    return jax.shard_map(
        body,
        mesh=grid,
        in_specs=(tokens, gain, gain, rows, rows, rows, columns, tokens),
        out_specs=(tokens, tokens, gain, gain, rows, rows, rows, columns),
        check_vma=False,
    )
```

```python
import functools
import math

import jax
import jax.numpy as jnp
from jax import lax
from jax.experimental import pallas as pl
from jax.experimental.pallas import tpu as pltpu
from jax.sharding import Mesh
from jax.sharding import PartitionSpec as P

HEADS = 16
norm_eps = 1e-05
rope_base = 160000.0
f32 = jnp.float32
bf16 = jnp.bfloat16
LANES = 128
MIB = 1024 * 1024


def partner(array, axis):
    return lax.ppermute(array, axis, [(0, 1), (1, 0)])


def opposite(array, axes):
    return lax.ppermute(array, axes, [(i, 3 - i) for i in range(4)])


def after(array, *others):
    return lax.optimization_barrier((array, *others))[0]


class Taken:
    def __init__(self, arrays):
        self._arrays = arrays

    def __getattr__(self, name):
        return self._arrays.pop(name)


class Live:
    def __init__(self):
        self._held, self._due = {}, {}

    def __getattr__(self, name):
        return self._held[name]

    def put(self, due, **arrays):
        self._held.update(arrays)
        self._due.update(dict.fromkeys(arrays, due))

    @property
    def take(self):
        return Taken(self._held)

    def fence(self, stage):
        names = [name for name in self._held if self._due[name] <= stage]
        arrays = lax.optimization_barrier(tuple(self._held[name] for name in names))
        self._held.update(zip(names, arrays))


ROUND_1, ROUND_2, ROUND_3, ATTEND, RETURN, MIDDLE, SPREAD, FEED, CHIP, COLLECT, MIDDLE_BACK, LEAVE, ATTEND_BACK, OVER_X, OVER_ZL, OVER_ZH, LAST = range(17)
ENTER = -1
SCHEDULE = dict(
    qkv_pack=(ENTER, ENTER),
    qkv_slices=(ROUND_1, ROUND_2),
    qkv_y=(ROUND_3, ROUND_3),
    qkv_whole=(ROUND_3, ROUND_3),
    feed_pack=(ROUND_1, ROUND_1),
    feed_slices=(ROUND_2, ROUND_2),
    feed_zh=(ATTEND, RETURN),
    feed_y=(ATTEND, RETURN),
    feed_far_y=(MIDDLE, SPREAD),
    feed_whole=(SPREAD, SPREAD),
    attn_y=(ROUND_1, ROUND_2),
    attn_zh=(ROUND_2, ROUND_2),
    attn_zl=(ROUND_3, ROUND_3),
    attn_x=(ATTEND, ATTEND),
    attn_whole=(RETURN, RETURN),
    cot_over_x=(ROUND_1, ROUND_1),
    cot_over_z=(ROUND_3, ATTEND),
    cot_over_zx=(RETURN, RETURN),
    cot_cores=(FEED, FEED),
    tables=(ROUND_1, ROUND_2),
    rest=(COLLECT, COLLECT),
    result_sums=(LEAVE, ATTEND_BACK),
    result_x=(LEAVE, ATTEND_BACK),
    result_z=(LEAVE, ATTEND_BACK),
    result_both=(LEAVE, ATTEND_BACK),
    result_out=(OVER_ZH, OVER_ZH),
    grad_in_y=(COLLECT, LEAVE),
    grad_in_zh=(OVER_X, OVER_ZL),
    grad_in_slices=(OVER_ZH, OVER_ZH),
    grad_attn_made=(LEAVE, LEAVE),
    grad_attn_cut=(LEAVE, LEAVE),
    grad_attn_y=(ATTEND_BACK, OVER_ZH),
    grad_attn_zl=(OVER_X, OVER_X),
    grad_attn_x=(OVER_ZL, OVER_ZL),
    grad_attn_zh=(OVER_ZH, OVER_ZH),
    grad_qkv_made=(OVER_X, OVER_X),
    grad_qkv_y=(OVER_ZL, OVER_ZL),
    grad_qkv_slices=(LAST, LAST),
)
FENCES = set(range(ENTER, LAST))


def name_of(kernel):
    return kernel.func.__name__ if isinstance(kernel, functools.partial) else kernel.__name__


def add(*terms):
    total = terms[0].astype(f32)
    for term in terms[1:]:
        total = total + term.astype(f32)
    return total.astype(terms[0].dtype)


def call(kernel, outs, places, *arrays, scratch=(), mib=16, flops=0, exps=0):
    vmem = pl.BlockSpec(memory_space=pltpu.VMEM)
    moved = sum(array.size * array.dtype.itemsize for array in arrays)
    moved += sum(math.prod(shape) * jnp.dtype(dtype).itemsize for shape, dtype in outs)
    return pl.pallas_call(
        kernel,
        in_specs=[pl.BlockSpec(memory_space=pltpu.SMEM)] + [vmem] * len(arrays),
        out_specs=[vmem] * len(outs),
        out_shape=[jax.ShapeDtypeStruct(shape, dtype) for shape, dtype in outs],
        scratch_shapes=list(scratch),
        compiler_params=pltpu.CompilerParams(vmem_limit_bytes=mib * MIB),
        cost_estimate=pl.CostEstimate(flops=flops, bytes_accessed=moved, transcendentals=exps),
        name=name_of(kernel),
    )(places, *arrays)


CHIP, ZH, ZL, X, C, Y = range(6)


def nt(left, right):
    return lax.dot_general(left, right, (((1,), (1,)), ((), ())), preferred_element_type=f32)


def tn(left, right):
    return lax.dot_general(left, right, (((0,), (0,)), ((), ())), preferred_element_type=f32)


def nn(left, right):
    return lax.dot_general(left, right, (((1,), (0,)), ((), ())), preferred_element_type=f32)


def normalize(values):
    centre = values - jnp.mean(values, axis=-1, keepdims=True)
    inverse = lax.rsqrt(jnp.mean(centre * centre, axis=-1, keepdims=True) + norm_eps)
    return centre * inverse, inverse


def normalize_back(scaled, normed, inverse):
    inner = jnp.mean(scaled * normed, axis=-1, keepdims=True)
    return inverse * (scaled - jnp.mean(scaled, axis=-1, keepdims=True) - normed * inner)


def pick_kernel(places, own_ref, other_ref, block_ref):
    half = own_ref.shape[1]
    block_ref[:half, :] = own_ref[places[C]]
    block_ref[half:, :] = other_ref[places[C]]


def enter_kernel(places, own_ref, other_ref, cot_a_ref, cot_b_ref, block_ref, cot_ref, low_ref):
    pick_kernel(places, own_ref, other_ref, block_ref)
    pick_kernel(places, cot_a_ref, cot_b_ref, cot_ref)
    low_ref[...] = normalize(block_ref[...].astype(f32))[0].astype(bf16)


def leave_kernel(places, own_ref, other_ref, out_ref):
    out_ref[places[C]] = own_ref[...]
    out_ref[1 - places[C]] = other_ref[...]


def assemble_kernel(lead, first, second, places, a_ref, b_ref, c_ref, d_ref, out_ref):
    chip = places[lead] if lead is not None else 0
    one, two = places[first], places[second]
    for i, row in enumerate(((a_ref, b_ref), (c_ref, d_ref))):
        for j, ref in enumerate(row):
            for at in range(ref.shape[0]):
                out_ref[chip ^ at, one ^ i, :, two ^ j] = ref[at]


def assemble(places, lead, first, second, pieces):
    extent = pieces[0].shape
    shape = (extent[0], 2, extent[1], 2) + extent[2:]
    if extent[2] % 16 == 0:
        kernel = functools.partial(assemble_kernel, lead, first, second)
        return call(kernel, [(shape, bf16)], places, *pieces)[0]

    def ordered(own, other, place, axis):
        straight = jnp.stack([own, other], axis)
        return jnp.where(place == 0, straight, jnp.flip(straight, axis))

    one = ordered(pieces[0], pieces[1], places[second], 2)
    two = ordered(pieces[2], pieces[3], places[second], 2)
    whole = ordered(one, two, places[first], 1)
    if lead is None:
        return whole
    return jnp.take(whole, jnp.arange(extent[0]) ^ places[lead], axis=0)


def assemble_rows_kernel(places, a_ref, b_ref, c_ref, d_ref, out_ref):
    for i, row in enumerate(((a_ref, b_ref), (c_ref, d_ref))):
        for j, ref in enumerate(row):
            for at in range(4):
                for k in range(2):
                    out_ref[places[CHIP] ^ (2 * at + j), places[C] ^ i, places[Y] ^ k] = ref[at, k]


def assemble_rows(places, pieces):
    if pieces[0].shape[2] % 16 == 0:
        shape = (8, 2) + pieces[0].shape[1:]
        return call(assemble_rows_kernel, [(shape, bf16)], places, *pieces)[0]
    merged = [jnp.stack(pieces[at : at + 2], axis=1) for at in (0, 2)]
    merged = [member.reshape((8, 1) + member.shape[2:]) for member in merged]
    pieces = [member[:, :, at] for member in merged for at in range(2)]
    return assemble(places, CHIP, C, Y, pieces)


def total_kernel(places, a_ref, b_ref, out_ref):
    out_ref[...] = (a_ref[...].astype(f32) + b_ref[...].astype(f32)).astype(bf16)


def total(places, kept, other):
    if kept.shape[1] % 16 == 0:
        return call(total_kernel, [(kept.shape, bf16)], places, kept, other)[0]
    return add(kept, other)


def put_shares(made, place, at, kept_ref, sent_ref):
    share, width = kept_ref.shape[1:]
    groups = made.shape[0] // (2 * share)
    made = made.reshape(groups, 2, share, width)
    kept_ref[pl.ds(at, groups)] = jnp.where(place == 0, made[:, 0], made[:, 1]).astype(bf16)
    sent_ref[pl.ds(at, groups)] = jnp.where(place == 0, made[:, 1], made[:, 0]).astype(bf16)


def split_kernel(which, count, places, *refs):
    kept_ref, sent_ref = refs[count:]
    place = places[which]
    for ref, at in ((kept_ref, place), (sent_ref, 1 - place)):
        total = refs[0][:, at]
        if count > 1:
            total = total.astype(f32)
            for term in refs[1:count]:
                total = total + term[:, at].astype(f32)
        ref[...] = total.astype(bf16)


def split(places, which, parts, before):
    shape = parts[0].shape
    rest = shape[:before] + shape[before + 1 :]
    if shape[-2] % 16 == 0:
        flat = (math.prod(shape[:before]), 2, math.prod(shape[before + 1 : -1]), shape[-1])
        outs = [((flat[0],) + flat[2:], bf16)] * 2
        kernel = functools.partial(split_kernel, which, len(parts))
        halves = call(kernel, outs, places, *[part.reshape(flat) for part in parts])
        return [half.reshape(rest) for half in halves]
    total = add(*parts)
    return [
        lax.dynamic_index_in_dim(total, at, before, False)
        for at in (places[which], 1 - places[which])
    ]


def halves_swapped(values, half):
    lane = lax.broadcasted_iota(jnp.int32, values.shape, 1)
    up = pltpu.roll(values, half, 1)
    down = pltpu.roll(values, values.shape[1] - half, 1)
    return jnp.where(lane % (2 * half) < half, down, up)


def project_kernel(half, places, *refs):
    pieces, (weight_ref, table_ref, out_ref, stack_ref) = refs[:8], refs[8:]
    width = out_ref.shape[1] // 3
    rows = pieces[0].shape[0]
    for at in range(0, 8, 2):
        here = pl.ds(at * rows, 2 * rows)
        both = jnp.concatenate([ref[...] for ref in pieces[at : at + 2]])
        stack_ref[here, :] = both
        made = nn(both, weight_ref[...])
        cosine, sine = table_ref[here, :width], table_ref[here, width:]
        for place in range(2):
            part = made[:, place * width : (place + 1) * width]
            turned = part * cosine + halves_swapped(part, half) * sine
            out_ref[here, place * width : (place + 1) * width] = turned.astype(bf16)
        out_ref[here, 2 * width :] = made[:, 2 * width :].astype(bf16)


def of_head(values, head, size):
    lane = lax.broadcasted_iota(jnp.int32, values.shape, 1)
    return jnp.where(lane // size == head, values, jnp.zeros_like(values))


def keys_and_values(refs, width):
    if len(refs) == 1:
        return refs[0][:, width : 2 * width], refs[0][:, 2 * width :]
    return refs[1][:, :width], refs[1][:, width:]


def attend_kernel(size, places, *refs):
    refs, (o_ref, log_ref) = refs[:-2], refs[-2:]
    block, width = o_ref.shape[1:]
    keys, values = keys_and_values(refs, width)
    step = log_ref.shape[2]
    scale = math.log2(math.e) / math.sqrt(size)

    def visit(i, carry):
        queries = refs[0][pl.ds(pl.multiple_of(i * step, step), step), :width]
        outs = []
        for head in range(width // size):
            scores = nt(keys, of_head(queries, head, size))
            top = jnp.max(scores, axis=0, keepdims=True)
            weights = jnp.exp2((scores - top) * scale)
            total = jnp.sum(weights, axis=0, keepdims=True)
            probs = (weights * (1.0 / total)).astype(bf16)
            outs.append(tn(values, probs)[head * size : (head + 1) * size])
            log_ref[i, head : head + 1, :] = top * scale + jnp.log2(total)
        out = jnp.transpose(jnp.concatenate(outs, axis=0)).astype(bf16)
        for at in range(step // block):
            chip = places[CHIP] ^ (i * (step // block) + at)
            o_ref[chip] = out[at * block : (at + 1) * block]
        return carry

    lax.fori_loop(0, refs[0].shape[0] // step, visit, 0)


def attend_back_kernel(size, together, places, *refs):
    refs, (grad_ref, log_ref, table_ref, dq_ref, dk_ref, dv_ref) = refs[:-6], refs[-6:]
    block, width = grad_ref.shape[1:]
    keys, values = keys_and_values(refs, width)
    step = log_ref.shape[2]
    scale = 1.0 / math.sqrt(size)
    exponent = scale * math.log2(math.e)
    dk_ref[...] = jnp.zeros_like(dk_ref)
    dv_ref[...] = jnp.zeros_like(dv_ref)

    def turned(part, here):
        back = halves_swapped(part, size // 2) * table_ref[here, width:]
        return (part * table_ref[here, :width] - back).astype(bf16)

    def visit(i, carry):
        here = pl.ds(pl.multiple_of(i * step, step), step)
        queries = refs[0][here, :width]
        grads = [grad_ref[places[CHIP] ^ (i * (step // block) + at)] for at in range(step // block)]
        grads = jnp.concatenate(grads)
        outs = []
        for head in range(width // size):
            query, grad = of_head(queries, head, size), of_head(grads, head, size)
            probs = jnp.exp2(nt(keys, query) * exponent - log_ref[i, head : head + 1, :])
            grad_probs = nt(values, grad)
            delta = jnp.sum(probs * grad_probs, axis=0, keepdims=True)
            grad_scores = (probs * (grad_probs - delta)).astype(bf16)
            outs.append(tn(keys, grad_scores)[head * size : (head + 1) * size])
            dk_ref[...] += nn(grad_scores, query)
            dv_ref[...] += nn(probs.astype(bf16), grad)
        dq = jnp.transpose(jnp.concatenate(outs, axis=0)) * scale
        dq_ref[here, :width] = turned(dq, here)
        return carry

    lax.fori_loop(0, refs[0].shape[0] // step, visit, 0)
    if together:
        everything = pl.ds(0, dq_ref.shape[0])
        dq_ref[:, width : 2 * width] = turned(dk_ref[...] * scale, everything)
        dq_ref[:, 2 * width :] = dv_ref[...].astype(bf16)
    else:
        dk_ref[...] = dk_ref[...] * scale


def turn_back_kernel(half, places, dq_ref, dk_ref, dv_ref, table_ref, out_ref):
    width = dq_ref.shape[1]
    part = dk_ref[...]
    back = halves_swapped(part, half) * table_ref[:, width:]
    out_ref[:, :width] = dq_ref[...]
    out_ref[:, width : 2 * width] = (part * table_ref[:, :width] - back).astype(bf16)
    out_ref[:, 2 * width :] = dv_ref[...].astype(bf16)


def middle_kernel(places, arrived_ref, weight_ref, tokens_ref, attended_ref, middle_ref, low_ref):
    wide = arrived_ref.shape[2]
    for at in range(arrived_ref.shape[0]):
        attended_ref[:, at * wide : (at + 1) * wide] = arrived_ref[at]
    middle = tokens_ref[...].astype(f32) + nn(attended_ref[...], weight_ref[...])
    middle_ref[...] = middle
    low_ref[...] = normalize(middle)[0].astype(bf16)


def feed_kernel(places, *refs):
    two, cot, (w_ref, hidden_ref, grad_ref), outs = refs[:8], refs[8:16], refs[16:19], refs[19:]
    piece = hidden_ref.shape[1]
    rows = two[0].shape[0]
    w_in, w_out = w_ref[:, : 2 * piece], w_ref[:, 2 * piece :]
    for at in (4, 6, 0, 2):
        here = pl.ds(at * rows, 2 * rows)
        gate_up = nn(jnp.concatenate([two[at][...], two[at + 1][...]]), w_in)
        grad_hidden = nn(jnp.concatenate([cot[at][...], cot[at + 1][...]]), w_out)
        gate, lift = gate_up[:, :piece], gate_up[:, piece:]
        cdf = 0.5 * (1.0 + lax.erf(gate * math.sqrt(0.5)))
        density = jnp.exp(-0.5 * gate * gate) * (1.0 / math.sqrt(2.0 * math.pi))
        activated = gate * cdf
        hidden_ref[here, :] = (activated * lift).astype(bf16)
        grad_gate = (grad_hidden * lift * (cdf + gate * density)).astype(bf16)
        grad_lift = (grad_hidden * activated).astype(bf16)
        grad_ref[here, :piece] = grad_gate
        grad_ref[here, piece:] = grad_lift
        made = nt(grad_gate, w_in[:, :piece]) + nt(grad_lift, w_in[:, piece:])
        outs[at // 4][pl.ds(at % 4 * rows, 2 * rows), :] = made.astype(bf16)


def feed(places, two, cot, weights):
    rows, width = two[0].shape
    piece = weights.shape[1] // 3
    outs = [((8 * rows, piece), bf16), ((8 * rows, 2 * piece), bf16)] + [((4 * rows, width), bf16)] * 2
    hidden, grads, *terms = call(
        feed_kernel,
        outs,
        places,
        *two,
        *cot,
        weights,
        mib=24,
        flops=80 * rows * width * piece,
        exps=16 * rows * piece,
    )
    return hidden, grads, terms


def feed_rest_kernel(places, *refs):
    two, cot, (hidden_ref, grad_ref, w_ref), outs, made_refs = (
        refs[:8],
        refs[8:16],
        refs[16:19],
        refs[19:21],
        refs[21:],
    )
    piece = hidden_ref.shape[1]
    rows, width = two[0].shape
    w_out = w_ref[:, 2 * piece :]
    for at in (4, 6, 0, 2):
        made = nt(hidden_ref[pl.ds(at * rows, 2 * rows), :], w_out)
        outs[at // 4][pl.ds(at % 4 * rows, 2 * rows), :] = made.astype(bf16)
    step = width // 4
    for at in range(0, width, step):
        here = pl.ds(at, step)
        left = jnp.concatenate([ref[:, here] for ref in two])
        made = tn(left, grad_ref[...])
        left = jnp.concatenate([ref[:, here] for ref in cot])
        made = jnp.concatenate([made, tn(left, hidden_ref[...])], axis=1)
        if len(made_refs) == 1:
            made_refs[0][here, :] = made.astype(bf16)
        else:
            put_shares(made, places[Y], at // (2 * made_refs[0].shape[1]), *made_refs)


def feed_rest(places, two, cot, hidden, grads, weights, shares):
    rows, width = two[0].shape
    outs = [((4 * rows, width), bf16)] * 2 + [(shape, bf16) for shape in shares]
    made = call(
        feed_rest_kernel,
        outs,
        places,
        *two,
        *cot,
        hidden,
        grads,
        weights,
        mib=24,
        flops=64 * rows * width * (weights.shape[1] // 3),
    )
    return made[:2], made[2:]


def chip_sums_kernel(places, a_ref, b_ref, *outs):
    rows = outs[0].shape[0]
    for at, ref in enumerate(outs):
        here = pl.ds(at * rows, rows)
        ref[...] = (a_ref[here, :].astype(f32) + b_ref[here, :].astype(f32)).astype(bf16)


def chip_sums(places, here, there):
    shape = (here.shape[0] // 4, here.shape[1])
    return call(chip_sums_kernel, [(shape, bf16)] * 4, places, here, partner(there, "c"))


def far_sums_kernel(places, kept_ref, across_ref, six_ref, four_ref):
    rows = six_ref.shape[0]
    for at, ref in enumerate((six_ref, four_ref)):
        here = pl.ds(at * rows, rows)
        ref[...] = (kept_ref[here, :].astype(f32) + across_ref[here, :].astype(f32)).astype(bf16)


def near_sums_kernel(places, kept_ref, across_ref, four_ref, both_ref, two_ref, own_ref, out_ref):
    far_sums_kernel(places, kept_ref, across_ref, two_ref, own_ref)
    out_ref[...] = (four_ref[...].astype(f32) + both_ref[...].astype(f32)).astype(bf16)


def result_kernel(places, middle_ref, a_ref, b_ref, c_ref, d_ref, kept_ref, sent_ref):
    total = middle_ref[...]
    for ref in (a_ref, b_ref, c_ref, d_ref):
        total = total + ref[...].astype(f32)
    total = total.astype(bf16)
    half = kept_ref.shape[0]
    kept_ref[...] = total[:half]
    sent_ref[...] = total[half:]


def middle_back_kernel(
    places, middle_ref, cot_ref, weight_ref, a_ref, b_ref, c_ref, d_ref, grad_ref, low_ref, leaving_ref
):
    scaled = a_ref[...].astype(f32)
    for ref in (b_ref, c_ref, d_ref):
        scaled = scaled + ref[...].astype(f32)
    normed, inverse = normalize(middle_ref[...])
    grad = cot_ref[...].astype(f32) + normalize_back(scaled, normed, inverse)
    grad_ref[...] = grad
    low = grad.astype(bf16)
    low_ref[...] = low
    made = nt(low, weight_ref[...]).astype(bf16)
    wide = leaving_ref.shape[2]
    for at in range(leaving_ref.shape[0]):
        leaving_ref[at] = made[:, at * wide : (at + 1) * wide]


def outer_kernel(places, left_ref, right_ref, *made_refs):
    made = tn(left_ref[...], right_ref[...])
    if len(made_refs) == 1:
        made_refs[0][...] = made.astype(bf16)
    else:
        put_shares(made, places[C], 0, *made_refs)


def project_back_kernel(places, grad_ref, weight_ref, *outs):
    rows = outs[0].shape[0] // 2
    for at in (6, 4, 2, 0):
        made = nt(grad_ref[pl.ds(at * rows, 2 * rows), :], weight_ref[...]).astype(bf16)
        first = 0 if at >= 4 else 2
        here = pl.ds((0 if at in (6, 2) else 1) * rows, rows)
        outs[first][here, :] = made[:rows]
        outs[first + 1][here, :] = made[rows:]


def project_outer_kernel(places, left_ref, grad_ref, *made_refs):
    width = left_ref.shape[1]
    step = width // 4
    for at in range(0, width, step):
        made = tn(left_ref[:, pl.ds(at, step)], grad_ref[...])
        if len(made_refs) == 1:
            made_refs[0][pl.ds(at, step), :] = made.astype(bf16)
        else:
            put_shares(made, places[C], at // (2 * made_refs[0].shape[1]), *made_refs)


def tokens_back_kernel(places, tokens_ref, grad_ref, a_ref, b_ref, c_ref, kept_ref, sent_ref):
    scaled = a_ref[...].astype(f32)
    for ref in (b_ref, c_ref):
        scaled = scaled + ref[...].astype(f32)
    normed, inverse = normalize(tokens_ref[...].astype(f32))
    total = grad_ref[...] + normalize_back(scaled, normed, inverse)
    half = kept_ref.shape[0]
    kept_ref[...] = total[:half]
    sent_ref[...] = total[half:]


def qkv_out_kernel(places, made_ref, weight_ref, gain_ref, out_ref, gain_grad_ref):
    pairs, rows, wide = made_ref.shape
    wide = wide // 3
    row = lax.broadcasted_iota(jnp.int32, (rows, rows), 0)
    lane = lax.broadcasted_iota(jnp.int32, (rows, rows), 1)
    gain = jnp.sum(jnp.where(row == lane, gain_ref[...].astype(f32), 0.0), axis=1, keepdims=True)
    total = jnp.zeros((rows, wide), f32)
    for at in range(pairs):
        for part in range(3):
            first = (part * pairs + at) * wide
            made = made_ref[at, :, part * wide : (part + 1) * wide].astype(f32)
            total = total + made * weight_ref[:, first : first + wide].astype(f32)
            out_ref[:, first : first + wide] = made * gain
    total = jnp.sum(total, axis=1, keepdims=True)
    gain_grad_ref[...] = jnp.sum(jnp.where(row == lane, total, 0.0), axis=0, keepdims=True)


def columns_by(array, pieces, piece):
    rows, count = array.shape
    padded = jnp.pad(array, ((0, 0), (0, pieces * piece - count)))
    return jnp.swapaxes(padded.reshape(rows, pieces, piece), 0, 1)


def columns_back(array, count):
    pieces, rows, piece = array.shape
    return jnp.swapaxes(array, 0, 1).reshape(rows, pieces * piece)[:, :count]


def body(inputs, gain_attn, gain_mlp, w_qkv, w_attn_out, w_in, w_out, cotangent):
    pairs, squares = 8, 8
    rings = lax.axis_size("r")
    seqs, half_block, width = inputs.shape
    owned = w_qkv.shape[0]
    size = width // HEADS
    half = size // 2
    wide = width // pairs
    block = seqs * half_block
    span = pairs * block
    ff = w_out.shape[0]
    piece = -(-ff // (squares * LANES)) * LANES
    chips, square = ("zh", "zl", "x"), ("zl", "x", "c")
    everyone = ("r",) + chips + ("c", "y")
    ri, zh, zl, xi, ci, yi = (lax.axis_index(name) for name in everyone)
    places = jnp.stack([4 * zh + 2 * zl + xi, zh, zl, xi, ci, yi]).astype(jnp.int32)
    block_low, half_low = ((block, width), bf16), ((half_block, width), bf16)
    block_full, half_full = ((block, width), f32), ((half_block, width), f32)

    def over_rings(array):
        return lax.all_gather(array, "r", axis=0) if rings > 1 else array

    def ring_sums(array):
        if rings > 1:
            return lax.psum_scatter(array, "r", scatter_dimension=0, tiled=True)
        return array

    gain_one = gain_attn.astype(f32)[:, None]
    gain_two = gain_mlp.astype(f32)[:, None]
    count = rings * span
    direct = rings == 1 and owned % 16 == 0

    live = Live()
    steps = []

    def step(made):
        steps.append((SCHEDULE[made.__name__], made))

    def begin(stage):
        for at, ((start, due), made) in enumerate(steps):
            if start == stage:
                steps[at] = ((None, due), made)
                live.put(due, **made())

    def reach(stage):
        begin(stage)
        if stage in FENCES:
            live.fence(stage)


    @step
    def qkv_pack():
        scaled = (live.take.w_qkv.astype(f32) * gain_one).astype(bf16)
        slices = scaled.reshape(owned, 3, pairs, wide).transpose(2, 0, 1, 3)
        return dict(slices=slices.reshape(pairs, owned, 3 * wide))

    @step
    def qkv_slices():
        return dict(qkv_own=lax.all_to_all(live.take.slices, chips, 0, 0, tiled=True)[:, None])

    @step
    def qkv_y():
        return dict(qkv_other=partner(live.qkv_own, "y"))

    @step
    def qkv_whole():
        parts = [live.take.qkv_own, live.take.qkv_other]
        parts = parts + [partner(part, "c") for part in parts]
        return dict(qkv=over_rings(assemble(places, None, C, Y, parts)).reshape(width, 3 * wide))


    @step
    def feed_pack():
        scaled = (live.take.w_in.astype(f32) * gain_two).astype(bf16)
        packed = [
            columns_by(scaled[:, :ff], squares, piece),
            columns_by(scaled[:, ff:], squares, piece),
            columns_by(jnp.transpose(live.take.w_out), squares, piece),
        ]
        return dict(packed=jnp.concatenate(packed, axis=2))

    @step
    def feed_slices():
        return dict(packed=lax.all_to_all(live.take.packed, square, 0, 0, tiled=True)[None])

    @step
    def feed_zh():
        return dict(packed_far=partner(live.packed, "zh"))

    @step
    def feed_y():
        return dict(packed_y=partner(live.packed, "y"))

    @step
    def feed_far_y():
        return dict(packed_far_y=partner(live.packed_far, "y"))

    @step
    def feed_whole():
        take = live.take
        parts = [take.packed, take.packed_y, take.packed_far, take.packed_far_y]
        whole = assemble(places, None, ZH, Y, parts)
        return dict(weights=over_rings(whole).reshape(width, 3 * piece))


    @step
    def attn_y():
        return dict(full=jnp.stack([live.w_attn_out, partner(live.take.w_attn_out, "y")]))

    @step
    def attn_zh():
        return dict(full=jnp.stack([live.full, partner(live.full, "zh")]))

    @step
    def attn_zl():
        return dict(full=jnp.stack([live.full, partner(live.full, "zl")], axis=1))

    @step
    def attn_x():
        return dict(full_x=partner(live.full, "x"))

    @step
    def attn_whole():
        parts = [part.reshape(4, 2, owned, width) for part in (live.take.full, live.take.full_x)]
        parts = parts + [partner(part, "c") for part in parts]
        return dict(attn=over_rings(assemble_rows(places, parts)).reshape(width, width))


    @step
    def cot_over_x():
        return dict(cot_x=partner(live.cot, "x"))

    @step
    def cot_over_z():
        return dict(cot_z=partner(live.cot, "zl"))

    @step
    def cot_over_zx():
        return dict(cot_zx=partner(live.cot_z, "x"))

    @step
    def cot_cores():
        parts = (live.cot, live.cot_x, live.cot_z, live.cot_zx)
        own, over_x, over_z, over_zx = (partner(part, "c") for part in parts)
        return dict(core=own, core_x=over_x, core_z=over_z, core_zx=over_zx)

    @step
    def tables():
        lane = jnp.arange(wide, dtype=jnp.int32)
        frequency = rope_base ** (-2.0 * (lane % half).astype(f32) / size)
        sign = jnp.where(lane % size < half, -1.0, 1.0)
        row = jnp.arange(span, dtype=jnp.int32)
        chip = (live.places[CHIP] ^ (row // block)) * block
        core = (live.places[C] ^ (row % block // half_block)) * half_block
        at = ri * span + chip + core + row % half_block
        angles = at.astype(f32)[:, None] * frequency[None, :]
        return dict(table=jnp.concatenate([jnp.cos(angles), jnp.sin(angles) * sign], axis=1))


    @step
    def rest():
        shape = (2 * squares, owned, 3 * piece)
        result, shares = feed_rest(
            places,
            all_two,
            all_cotangent(),
            live.take.hidden,
            live.take.gate_up,
            live.take.weights,
            [shape] * 2 if direct else [(width, 3 * piece)],
        )
        if not direct:
            terms = ring_sums(shares[0]).reshape(2 * squares, 2, owned, 3 * piece)
            shares = split(places, Y, [terms], 1)
        return dict(
            result_here=result[0],
            result_there=result[1],
            weights_kept=shares[0],
            weights_sent=shares[1],
        )

    @step
    def result_sums():
        sums = chip_sums(places, live.take.result_here, live.take.result_there)
        return dict(result0=sums[0], result1=sums[1], result2=sums[2], result3=sums[3])

    @step
    def result_x():
        return dict(result1=partner(live.result1, "x"))

    @step
    def result_z():
        return dict(result2=partner(live.result2, "zl"))

    @step
    def result_both():
        return dict(result3=opposite(live.result3, ("zl", "x")))

    @step
    def result_out():
        take = live.take
        kept, sent = call(
            result_kernel,
            [half_low] * 2,
            places,
            live.middle,
            take.result0,
            take.result1,
            take.result2,
            take.result3,
        )
        out = call(leave_kernel, [(inputs.shape, bf16)], places, kept, partner(sent, "c"))[0]
        return dict(output=out)

    @step
    def grad_in_y():
        return dict(weights_y=partner(live.take.weights_sent, "y"))

    @step
    def grad_in_zh():
        shares = [live.take.weights_kept, live.take.weights_y]
        shares = [share.reshape(1, 2, squares * owned, 3 * piece) for share in shares]
        kept, sent = split(places, ZH, shares, 1)
        return dict(weights_kept=kept, weights_far=partner(sent, "zh"))

    @step
    def grad_in_slices():
        shares = [live.take.weights_kept, live.take.weights_far]
        shares = [share.reshape(squares, owned, 3 * piece) for share in shares]
        return dict(grad_packed=lax.all_to_all(total(places, *shares), square, 0, 0, tiled=True))


    @step
    def grad_attn_made():
        shape = (pairs, 2 * owned, width)
        shares = call(
            outer_kernel,
            [(shape, bf16)] * 2 if direct else [((width, width), bf16)],
            places,
            live.take.attended,
            live.take.branch,
        )
        if not direct:
            terms = ring_sums(shares[0]).reshape(pairs, 2, 2 * owned, width)
            shares = split(places, C, [terms], 1)
        return dict(attn_kept=shares[0], attn_other=partner(shares[1], "c"))

    def attn_sums(which, before, after_it, name):
        shares = [live.take.attn_kept, live.take.attn_other]
        shares = [share.reshape(before, 2, after_it * owned, width) for share in shares]
        kept, sent = split(places, which, shares, 1)
        return dict(attn_kept=kept, attn_other=partner(sent, name))

    @step
    def grad_attn_cut():
        shares = [live.take.attn_kept, live.take.attn_other]
        shares = [share.reshape(8, 2, owned, width) for share in shares]
        kept, sent = split(places, Y, shares, 1)
        return dict(attn_kept=kept, attn_sent=sent)

    @step
    def grad_attn_y():
        return dict(attn_other=partner(live.take.attn_sent, "y"))

    @step
    def grad_attn_zl():
        return attn_sums(ZL, 2, 2, "zl")

    @step
    def grad_attn_x():
        return attn_sums(X, 2, 1, "x")

    @step
    def grad_attn_zh():
        return attn_sums(ZH, 1, 1, "zh")


    @step
    def grad_qkv_made():
        shape = (pairs, 2 * owned, 3 * wide)
        shares = call(
            project_outer_kernel,
            [(shape, bf16)] * 2 if direct else [((width, 3 * wide), bf16)],
            places,
            all_one,
            live.take.projected,
        )
        if not direct:
            terms = ring_sums(shares[0]).reshape(pairs, 2, 2 * owned, 3 * wide)
            shares = split(places, C, [terms], 1)
        shares = [shares[0], partner(shares[1], "c")]
        shares = [share.reshape(pairs, 2, owned, 3 * wide) for share in shares]
        kept, sent = split(places, Y, shares, 1)
        return dict(qkv_kept=kept, qkv_sent=sent)

    @step
    def grad_qkv_y():
        return dict(qkv_kept=total(places, live.take.qkv_kept, partner(live.take.qkv_sent, "y")))

    @step
    def grad_qkv_slices():
        return dict(grad_qkv=lax.all_to_all(live.take.qkv_kept, chips, 0, 0, tiled=True))

    tokens, cot, low_one = call(
        enter_kernel,
        [block_low] * 3,
        places,
        inputs,
        partner(inputs, "c"),
        cotangent,
        partner(cotangent, "c"),
    )
    live.put(-1, tokens=tokens, cot=cot, one0=low_one, places=places)
    live.put(-1, w_qkv=w_qkv, w_attn_out=w_attn_out, w_in=w_in, w_out=w_out)
    reach(-1)

    one1, one2, one4 = (partner(live.one0, name) for name in ("x", "zl", "zh"))
    live.put(ROUND_1, one1=one1, one2=one2, one4=one4)
    reach(ROUND_1)
    places = live.places

    one3, one5, one6 = partner(live.one2, "x"), partner(live.one4, "x"), partner(live.one4, "zl")
    live.put(ROUND_2, one3=one3, one5=one5, one6=one6)
    reach(ROUND_2)

    live.put(ROUND_3, one7=partner(live.one6, "x"))
    reach(ROUND_3)

    take = live.take
    parts = [take.one0, take.one1, take.one2, take.one3, take.one4, take.one5, take.one6, take.one7]
    projected, all_one = call(
        functools.partial(project_kernel, half),
        [((span, 3 * wide), bf16), ((span, width), bf16)],
        places,
        *parts,
        live.qkv,
        live.table,
    )
    projected = [projected]
    if rings > 1:
        projected += [lax.all_gather(projected[0][:, wide:], "r", axis=0, tiled=True)]
    rows = 2 * block if count <= 2048 else block
    heads_out, logs = call(
        functools.partial(attend_kernel, size),
        [((pairs, block, wide), bf16), ((span // rows, 8, rows), f32)],
        places,
        *projected,
        mib=24,
    )
    live.put(ATTEND, heads=heads_out)
    reach(ATTEND)

    live.put(RETURN, arrived=lax.all_to_all(live.take.heads, chips, 0, 0, tiled=True))
    reach(RETURN)

    attended, middle, low_two = call(
        middle_kernel,
        [block_low, block_full, block_low],
        places,
        live.take.arrived,
        live.attn,
        live.tokens,
    )
    live.put(MIDDLE, attended=attended, middle=middle, two=low_two)
    reach(MIDDLE)

    over_x, over_z = partner(live.two, "x"), partner(live.two, "zl")
    live.put(SPREAD, over_x=over_x, over_z=over_z, over_both=opposite(live.two, ("zl", "x")))
    reach(SPREAD)

    def all_cotangent():
        here = [live.cot, live.cot_x, live.cot_z, live.cot_zx]
        return here + [live.core, live.core_x, live.core_z, live.core_zx]

    all_two = [live.take.two, live.take.over_x, live.take.over_z, live.take.over_both]
    all_two += [partner(member, "c") for member in all_two]
    begin(FEED)
    hidden, grad_gate_up, terms = feed(places, all_two, all_cotangent(), live.weights)
    live.put(FEED, hidden=hidden, gate_up=grad_gate_up, here=terms[0], there=terms[1])
    reach(FEED)

    sums = chip_sums(places, live.take.here, live.take.there)
    live.put(CHIP, sum0=sums[0], sum1=sums[1], sum2=sums[2], sum3=sums[3])
    reach(CHIP)

    over_both = opposite(live.take.sum3, ("zl", "x"))
    over_x, over_z = partner(live.take.sum1, "x"), partner(live.take.sum2, "zl")
    live.put(COLLECT, sum1=over_x, sum2=over_z, sum3=over_both)
    reach(COLLECT)

    take = live.take
    grad_middle, grad_branch, leaving = call(
        middle_back_kernel,
        [block_full, block_low, ((pairs, block, wide), bf16)],
        places,
        live.middle,
        live.cot,
        live.attn,
        take.sum0,
        take.sum1,
        take.sum2,
        take.sum3,
    )
    live.put(MIDDLE_BACK, grad_middle=grad_middle, branch=grad_branch, leaving=leaving)
    reach(MIDDLE_BACK)

    live.put(LEAVE, grad_heads=lax.all_to_all(live.take.leaving, chips, 0, 0, tiled=True))
    reach(LEAVE)

    kernel = functools.partial(attend_back_kernel, size, rings == 1)
    parts = projected + [live.take.grad_heads, logs, live.table]
    if rings == 1:
        grad_projected = call(
            kernel,
            [((span, 3 * wide), bf16)],
            places,
            *parts,
            scratch=[pltpu.VMEM((count, wide), f32)] * 2,
            mib=24,
        )[0]
    else:
        outs = [((span, wide), bf16), ((count, wide), f32), ((count, wide), f32)]
        grad_q, grad_k, grad_v = call(kernel, outs, places, *parts, mib=36)
        grad_projected = call(
            functools.partial(turn_back_kernel, half),
            [((span, 3 * wide), bf16)],
            places,
            grad_q,
            ring_sums(grad_k),
            ring_sums(grad_v),
            live.table,
        )[0]
    terms = call(
        project_back_kernel, [((2 * block, width), bf16)] * 4, places, grad_projected, live.qkv
    )
    live.put(ATTEND_BACK, projected=grad_projected, kept_far=terms[0], sent_far=terms[1])
    live.put(ATTEND_BACK, kept_near=terms[2], sent_near=terms[3])
    reach(ATTEND_BACK)

    over_x = partner(live.take.sent_far, "x")
    six, four = call(far_sums_kernel, [block_low] * 2, places, live.take.kept_far, over_x)
    live.put(OVER_X, six=six, four=four)
    reach(OVER_X)

    both = partner(live.take.six, "zl")
    over_x = partner(live.take.sent_near, "x")
    two, own, four = call(
        near_sums_kernel,
        [block_low] * 3,
        places,
        live.take.kept_near,
        over_x,
        live.take.four,
        both,
    )
    live.put(OVER_ZL, two=two, own=own, four=four)
    reach(OVER_ZL)

    live.put(OVER_ZH, far=partner(live.take.four, "zh"), near=partner(live.take.two, "zl"))
    reach(OVER_ZH)

    kept, sent = call(
        tokens_back_kernel,
        [half_full] * 2,
        places,
        live.tokens,
        live.grad_middle,
        live.own,
        live.near,
        live.far,
    )
    input_grad = call(leave_kernel, [(inputs.shape, f32)], places, kept, partner(sent, "c"))[0]
    reach(LAST)

    grad_attn = (live.attn_kept.astype(f32) + live.attn_other.astype(f32))[0]
    if owned % 16 == 0:
        grad_qkv, grad_gain_attn = call(
            qkv_out_kernel,
            [((owned, 3 * width), f32), ((1, owned), f32)],
            places,
            live.grad_qkv,
            w_qkv,
            gain_attn[None, :],
        )
        grad_gain_attn = grad_gain_attn[0]
    else:
        grad_qkv = live.grad_qkv.astype(f32).reshape(pairs, owned, 3, wide)
        grad_qkv = grad_qkv.transpose(1, 2, 0, 3).reshape(owned, 3 * width)
        grad_gain_attn = jnp.sum(grad_qkv * w_qkv.astype(f32), axis=1)
        grad_qkv = grad_qkv * gain_one

    grad_packed = live.grad_packed.astype(f32)
    grad_in = jnp.concatenate(
        [
            columns_back(grad_packed[:, :, :piece], ff),
            columns_back(grad_packed[:, :, piece : 2 * piece], ff),
        ],
        axis=1,
    )
    grad_out = jnp.transpose(columns_back(grad_packed[:, :, 2 * piece :], ff))
    grad_gain_mlp = jnp.sum(grad_in * w_in.astype(f32), axis=1)
    grad_in = grad_in * gain_two
    return (
        live.output,
        input_grad,
        grad_gain_attn,
        grad_gain_mlp,
        grad_qkv,
        grad_attn,
        grad_in,
        grad_out,
    )


def solution(mesh):
    ctx, fsdp = mesh.shape["ctx"], mesh.shape["fsdp"]
    everyone = ("r", "zh", "zl", "x", "c", "y")
    grid = Mesh(mesh.devices.reshape(ctx // 16, 2, 2, 2, 2, fsdp), everyone)
    tokens = P("y", everyone[:-1], None)
    gain, rows, columns = P(everyone), P(everyone, None), P(None, everyone)
    return jax.shard_map(
        body,
        mesh=grid,
        in_specs=(tokens, gain, gain, rows, rows, rows, columns, tokens),
        out_specs=(tokens, tokens, gain, gain, rows, rows, rows, columns),
        check_vma=False,
    )
```
